256 devices in a mesh: dp: 32 (over y, z_lo, core), dap: 8 (over z_hi, x).
Axes of the slice: x: 4, y: 4, z: 8 (z_hi: 2, z_lo: 4; z = z_hi * 4 + z_lo), core: 2. Of those that a mesh axis runs over, the one named last changes fastest.
Arguments:
- pair: bfloat16 [32, 128, 128, 128], P('dp', 'dap'), may hold values from -6 to 6
- pair_mask: int32 [32, 128, 128], P('dp', 'dap'), may hold values 0 or 1
- cotangent: bfloat16 [32, 128, 128, 128], P('dp', 'dap'), may hold values from -6 to 6
- w_in: bfloat16 [128, 640], replicated, may hold values from -0.5 to 0.5
- w_out: bfloat16 [128, 128], replicated, may hold values from -0.5 to 0.5
Outputs:
- update: bfloat16 [32, 128, 128, 128], P('dp', 'dap')
- grad_pair: bfloat16 [32, 128, 128, 128], P('dp', 'dap')
- grad_w_in: float32 [128, 640], replicated
- grad_w_out: float32 [128, 128], replicated
The draws below stay inside these ranges and needn't reach their ends.
All inputs are finite; a program needn't handle non-finite values. No bound on the sum of `pair_mask` on one device may be relied on, other than what follows from the above.
Results may differ from the reference program's by a relative error of at most 0.013.
Values may be sent and summed in bfloat16 or wider, within the bound.
A program may use at most 128 MiB of HBM per device.

```python
import jax
import jax.numpy as jnp
from jax import lax

C = 128
NRES = 128
CROPS = 32


def place_ends(values, stream_key, low, high):
    longest = values.shape.index(max(values.shape))
    spots = []
    for shift in (0, 1):
        where = [jax.random.randint(jax.random.fold_in(stream_key, axis), (), 0, length) for axis, length in enumerate(values.shape)]
        where[longest] = (where[longest] + shift) % values.shape[longest]
        spots.append(tuple(where))
    return values.at[spots[0]].set(low).at[spots[1]].set(high)


def block_scale(own_key, shape, split, smallest, high):
    level = 1.0
    for axis_at, parts in split:
        heights = jax.random.uniform(jax.random.fold_in(jax.random.fold_in(own_key, 6), axis_at), (parts,), jnp.float32, smallest / len(split), high / len(split))
        level = level * jnp.repeat(jnp.exp(heights), shape[axis_at] // parts).reshape((-1,) + (1,) * (len(shape) - 1 - axis_at))
    return level


def normal_values(rng, extent, scale, limit, pieces=(), kind=jnp.bfloat16):
    array = scale * jax.random.normal(rng, extent, jnp.float32)
    if pieces:
        array = array * block_scale(rng, extent, pieces, -0.22, 0.18)
    return jnp.clip(array, -limit, limit).astype(kind)


def setup_inputs(seed: int = 0) -> dict:
    keys = jax.random.split(jax.random.key(seed), 6)
    pair = normal_values(keys[0], (CROPS, NRES, NRES, C), 1.0, 6.0, ((0, 32), (1, 8)))
    pair_mask = place_ends((jax.random.randint(keys[1], (CROPS, NRES, NRES), 0, 10) < 9).astype(jnp.int32), jax.random.fold_in(keys[1], 1), 0, 1)
    cotangent = normal_values(keys[2], (CROPS, NRES, NRES, C), 1.0, 6.0, ((0, 32), (1, 8)))
    w_in = normal_values(keys[3], (C, 5 * C), C ** -0.5, 0.5)
    w_out = normal_values(keys[4], (C, C), C ** -0.5, 0.5)
    return dict(pair=pair, pair_mask=pair_mask, cotangent=cotangent, w_in=w_in, w_out=w_out)


EPS = 1e-05

def normalize(values):
    center = values - lax.optimization_barrier(jnp.mean(values, axis=-1, keepdims=True))
    scale = lax.rsqrt(lax.optimization_barrier(jnp.mean(center * center, axis=-1, keepdims=True)) + EPS)
    return (center * scale, scale)

def norm_back(grad_in, normed, scale):
    mean_grad = lax.optimization_barrier(jnp.mean(grad_in, axis=-1, keepdims=True))
    mean_prod = lax.optimization_barrier(jnp.mean(grad_in * normed, axis=-1, keepdims=True))
    return scale * (grad_in - mean_grad - normed * mean_prod)

def matmul(left, right):
    flat = left.reshape(-1, left.shape[-1])
    result = jnp.dot(flat, right, preferred_element_type=jnp.float32)
    return result.reshape(left.shape[:-1] + (right.shape[-1],))

def weight_grad(left, right):
    flat_left = left.reshape(-1, left.shape[-1])
    flat_right = right.reshape(-1, right.shape[-1])
    return jnp.dot(flat_left.T, flat_right, preferred_element_type=jnp.float32)

def one_crop(pair, mask, cotangent, w_in, w_out):
    width = pair.shape[-1]
    normed_in, scale_in = normalize(pair.astype(jnp.float32))
    normed_bf = normed_in.astype(jnp.bfloat16)
    project = matmul(normed_bf, w_in)
    left_gate = jax.nn.sigmoid(project[..., :width])
    left_values = project[..., width:2 * width]
    right_gate = jax.nn.sigmoid(project[..., 2 * width:3 * width])
    right_values = project[..., 3 * width:4 * width]
    out_gate = jax.nn.sigmoid(project[..., 4 * width:])
    masked = mask.astype(jnp.float32)[..., None]
    left = (left_gate * left_values * masked).astype(jnp.bfloat16)
    right = (right_gate * right_values * masked).astype(jnp.bfloat16)
    triangle = jnp.einsum('ikc,jkc->ijc', left.astype(jnp.float32), right.astype(jnp.float32))
    tri_normed, tri_scale = normalize(triangle)
    tri_bf = tri_normed.astype(jnp.bfloat16)
    output = matmul(tri_bf, w_out)
    update = (out_gate * output).astype(jnp.bfloat16)
    grad_update = cotangent.astype(jnp.float32)
    grad_output = (grad_update * out_gate).astype(jnp.bfloat16)
    grad_outgate = grad_update * output * out_gate * (1.0 - out_gate)
    grad_wout = weight_grad(tri_bf, grad_output)
    grad_tri = norm_back(matmul(grad_output, w_out.T), tri_normed, tri_scale).astype(jnp.bfloat16)
    grad_left = jnp.einsum('ijc,jkc->ikc', grad_tri.astype(jnp.float32), right.astype(jnp.float32))
    grad_right = jnp.einsum('ijc,ikc->jkc', grad_tri.astype(jnp.float32), left.astype(jnp.float32))
    grad_project = jnp.concatenate([grad_left * left_values * masked * left_gate * (1.0 - left_gate), grad_left * left_gate * masked, grad_right * right_values * masked * right_gate * (1.0 - right_gate), grad_right * right_gate * masked, grad_outgate], axis=-1).astype(jnp.bfloat16)
    grad_win = weight_grad(normed_bf, grad_project)
    grad_pair = norm_back(matmul(grad_project, w_in.T), normed_in, scale_in).astype(jnp.bfloat16)
    return (update, grad_pair, grad_win, grad_wout)

def reference(pair, pair_mask, cotangent, w_in, w_out):

    def step(carry, crop):
        update, grad_pair, grad_win, grad_wout = one_crop(crop[0], crop[1], crop[2], w_in, w_out)
        return ((carry[0] + grad_win, carry[1] + grad_wout), (update, grad_pair))
    start = (jnp.zeros(w_in.shape, jnp.float32), jnp.zeros(w_out.shape, jnp.float32))
    totals, outputs = lax.scan(step, start, (pair, pair_mask, cotangent))
    sum_in, sum_out = totals
    squares = jnp.sum(sum_in * sum_in) + jnp.sum(sum_out * sum_out)
    count = sum_in.size + sum_out.size
    clip = jnp.minimum(jnp.float32(1.0), lax.rsqrt(squares / count + 1e-06))
    return (outputs[0], outputs[1], sum_in * clip, sum_out * clip)
```

```python
import functools

import jax
import jax.numpy as jnp
from jax import lax
from jax.experimental import pallas as pl
from jax.experimental.pallas import tpu as pltpu
from jax.sharding import PartitionSpec as P

EPS = 1e-05
MESH = pl.DeviceIdType.MESH
F32 = jnp.float32
BF16 = jnp.bfloat16

C = 128
N = 128
ROWS = 16
CH = 16
WIDE = ROWS * N
GROUP = 4
NG = CH // GROUP
PEERS = 7


def dot(a, b):
    return lax.dot_general(a, b, (((1,), (0,)), ((), ())), preferred_element_type=F32)


def dot_nt(a, b):
    return lax.dot_general(a, b, (((1,), (1,)), ((), ())), preferred_element_type=F32)


def dot_tn(a, b):
    return lax.dot_general(a, b, (((0,), (0,)), ((), ())), preferred_element_type=F32)


def sigmoid(v):
    return 1.0 / (1.0 + jnp.exp(-v))


def mean0(v):
    return jnp.sum(v, axis=0, keepdims=True) * (1.0 / C)


def lanes(chunk, width):
    return pl.ds(pl.multiple_of(chunk * width, width), width)


def remote(src, dst, send_sem, recv_sem, device):
    return pltpu.make_async_remote_copy(
        src_ref=src, dst_ref=dst, send_sem=send_sem, recv_sem=recv_sem, device_id=device, device_id_type=MESH
    )


def kernel(
    pair, mask, cot, win, wout, upd, gpair, gwin, gwout,
    wt4, wog, woutt, xhat, xbf, scin, stage, stage2, send_l, send_r, recv_l, recv_r,
    al, bl, ar, br, ogs, a2, got, dt, tbt, gpt,
    tri, tri_r, send_g, recv_g, grad, gl, gr, gl_r, gr_r, wg, part1, part2, piece, mine, part3, half, part4,
    s_l, r_l, s_r, r_r, s_t, r_t, s_g, r_g, s_gl, r_gl, s_gr, r_gr, s_w, r_w,
):
    dp, me = lax.axis_index("dp"), lax.axis_index("dap")
    zh, x = me // 4, me % 4
    y, zlo, core = dp // 8, (dp // 2) % 4, dp % 2

    def row_peer(step):
        return ((zh + 1 - step // 4) % 2) * 4 + (x + step + 1) % 4

    my_xy = y * 4 + x

    def xy_peer(shift):
        other = (my_xy + shift) % 16
        return other, (((other // 4) * 4 + zlo) * 2 + core, zh * 4 + other % 4)

    z = zh * 4 + zlo
    my_zc = z * 2 + core

    def zc_peer(shift):
        other = (my_zc + shift) % 16
        oz = other // 2
        return other, ((y * 4 + oz % 4) * 2 + other % 2, (oz // 4) * 4 + x)

    barrier = pltpu.get_barrier_semaphore()

    def greet(shift, _):
        pl.semaphore_signal(barrier, inc=1, device_id=xy_peer(shift)[1], device_id_type=MESH)
        pl.semaphore_signal(barrier, inc=1, device_id=zc_peer(shift)[1], device_id_type=MESH)
        return 0

    lax.fori_loop(1, 16, greet, 0)
    for step in range(3):
        pl.semaphore_signal(barrier, inc=1, device_id=(dp, row_peer(step)), device_id_type=MESH)

    for b in range(5):
        block = win[:, b * C : (b + 1) * C].astype(F32).T.astype(BF16)
        if b == 4:
            wog[...] = block
        else:
            for e in range(8):
                wt4[e, b * CH : (b + 1) * CH, :] = block[e * CH : (e + 1) * CH, :]
    woutt[...] = wout[...].astype(F32).T.astype(BF16)

    def norm_pair(i, _):
        v = pair[i].astype(F32).T
        cen = v - mean0(v)
        sc = lax.rsqrt(mean0(cen * cen) + EPS)
        xh = cen * sc
        at = lanes(i, N)
        xhat[:, at] = xh
        xbf[:, at] = xh.astype(BF16)
        scin[:, at] = sc
        return 0

    lax.fori_loop(0, ROWS, norm_pair, 0, unroll=2)

    def project(e):
        for n in range(4):
            at = slice(n * 4 * N, (n + 1) * 4 * N)
            p = dot(wt4[e], xbf[:, at])
            m = jnp.concatenate([mask[4 * n + q : 4 * n + q + 1, :] for q in range(4)], axis=1).astype(F32)
            rows = pl.ds(pl.multiple_of(e * CH, CH), CH)
            for side, (ga, gb, st) in enumerate(((al, bl, stage), (ar, br, stage2))):
                s = sigmoid(p[2 * side * CH : (2 * side + 1) * CH])
                sm = s * m
                v = sm * p[(2 * side + 1) * CH : (2 * side + 2) * CH]
                ga[rows, at] = sm
                gb[rows, at] = v * (1.0 - s)
                for q in range(4):
                    st[pl.ds(4 * n + q, CH, stride=ROWS), :] = v[:, q * N : (q + 1) * N]
        lo = stage[...].astype(BF16).reshape(CH, ROWS, N)
        ro = stage2[...].astype(BF16).reshape(CH, ROWS, N)
        return lo, ro

    my_rows = pl.ds(pl.multiple_of(me * ROWS, ROWS), ROWS)
    my_ch = pl.multiple_of(me * CH, CH)

    def copy_lr(step):
        e = row_peer(step)
        return (
            remote(send_l.at[e], recv_l.at[:, my_rows, :], s_l.at[step], r_l.at[step], (dp, e)),
            remote(send_r.at[e], recv_r.at[:, my_rows, :], s_r.at[step], r_r.at[step], (dp, e)),
        )

    def send_lr(step, _):
        e = row_peer(step)
        lo, ro = project(e)
        send_l[e] = lo
        send_r[e] = ro
        for cp in copy_lr(step):
            cp.start()
        return 0

    pl.semaphore_wait(barrier, 33)
    lax.fori_loop(0, PEERS, send_lr, 0)
    lo, ro = project(me)
    recv_l[:, my_rows, :] = lo
    recv_r[:, my_rows, :] = ro

    def gate(n, _):
        at = lanes(n, 2 * N)
        og = sigmoid(dot(wog[...], xbf[:, at]))
        g = jnp.concatenate([cot[2 * n].astype(F32).T, cot[2 * n + 1].astype(F32).T], axis=1)
        go = g * og
        gob = go.astype(BF16)
        ogs[:, at] = og
        a2[:, at] = go * (1.0 - og)
        got[:, at] = gob
        dt[:, at] = dot(wout[...], gob)
        return 0

    lax.fori_loop(0, ROWS // 2, gate, 0)

    def wait_lr(step, _):
        for cp in copy_lr(step):
            cp.wait_recv()
        return 0

    lax.fori_loop(0, PEERS, wait_lr, 0)

    def copy_back(src, dst, ss, rs, g, step):
        e = row_peer(step)
        cs = pl.multiple_of(g * GROUP, GROUP)
        return remote(
            src.at[pl.ds(cs, GROUP), pl.ds(pl.multiple_of(e * ROWS, ROWS), ROWS), :],
            dst.at[pl.ds(my_ch + cs, GROUP), :, :],
            ss.at[step, g], rs.at[step, g], (dp, e),
        )

    def back(make, src, dst, ss, rs):
        def group(g, _):
            for q in range(GROUP):
                c = g * GROUP + q
                src[c] = make(c).astype(BF16)
            cs = pl.multiple_of(g * GROUP, GROUP)

            def start(step, _):
                copy_back(src, dst, ss, rs, g, step).start()
                return 0

            lax.fori_loop(0, PEERS, start, 0)
            dst[pl.ds(my_ch + cs, GROUP)] = src[pl.ds(cs, GROUP), my_rows, :]
            return 0

        lax.fori_loop(0, NG, group, 0)

    def back_wait(src, dst, ss, rs):
        def wait(t, _):
            copy_back(src, dst, ss, rs, t % NG, t // NG).wait_recv()
            return 0

        lax.fori_loop(0, PEERS * NG, wait, 0)

    def widen(src):
        def part(t, _):
            stage_rows = pl.ds(pl.multiple_of(t * N, N), N)
            half[stage_rows, :] = src[pl.ds(pl.multiple_of(t * 8, 8), 8)].astype(F32).reshape(N, N)
            return 0

        lax.fori_loop(0, ROWS, part, 0, unroll=2)

    back(lambda c: dot_nt(recv_l[c], recv_r[c]), tri, tri_r, s_t, r_t)
    back_wait(tri, tri_r, s_t, r_t)
    widen(tri_r)

    def rows_step(n, _):
        at = lanes(n, 2 * N)
        t = jnp.concatenate([half[pl.ds(2 * n + q, C, stride=ROWS), :] for q in range(2)], axis=1)
        cen = t - mean0(t)
        sc = lax.rsqrt(mean0(cen * cen) + EPS)
        tn = cen * sc
        tb = tn.astype(BF16)
        tbt[:, at] = tb
        out = dot(woutt[...], tb)
        u = ogs[:, at] * out
        gpt[4 * C :, at] = (a2[:, at] * out).astype(BF16)
        d = dt[:, at]
        gt = sc * (d - mean0(d) - tn * mean0(d * tn))
        for q in range(2):
            upd[2 * n + q] = u[:, q * N : (q + 1) * N].T.astype(BF16)
            grad[pl.ds(2 * n + q, C, stride=ROWS), :] = gt[:, q * N : (q + 1) * N]
        return 0

    lax.fori_loop(0, ROWS // 2, rows_step, 0)

    def copy_g(step):
        e = row_peer(step)
        return remote(send_g.at[e], recv_g.at[:, my_rows, :], s_g.at[step], r_g.at[step], (dp, e))

    def narrow(e):
        rows = pl.ds(pl.multiple_of(e * CH * ROWS, CH * ROWS), CH * ROWS)
        return grad[rows, :].astype(BF16).reshape(CH, ROWS, N)

    def start_g(step, _):
        e = row_peer(step)
        send_g[e] = narrow(e)
        copy_g(step).start()
        return 0

    lax.fori_loop(0, PEERS, start_g, 0)
    recv_g[:, my_rows, :] = narrow(me)

    wg[5 * C :, :] = dot_nt(tbt[...], got[...])
    wg[4 * C : 5 * C, :] = dot_nt(gpt[4 * C :, :], xbf[...])

    def wait_g(step, _):
        copy_g(step).wait_recv()
        return 0

    lax.fori_loop(0, PEERS, wait_g, 0)

    back(lambda c: dot(recv_g[c], recv_r[c]), gl, gl_r, s_gl, r_gl)
    back(lambda c: dot_tn(recv_g[c], recv_l[c]), gr, gr_r, s_gr, r_gr)

    for b, (src, dst, ss, rs, ga, gb) in enumerate(
        ((gl, gl_r, s_gl, r_gl, al, bl), (gr, gr_r, s_gr, r_gr, ar, br))
    ):
        back_wait(src, dst, ss, rs)
        widen(dst)

        def project_grad(n, _):
            at = lanes(n, 2 * N)
            t = jnp.concatenate([half[pl.ds(2 * n + q, C, stride=ROWS), :] for q in range(2)], axis=1)
            gpt[2 * b * C : (2 * b + 1) * C, at] = (t * gb[:, at]).astype(BF16)
            gpt[(2 * b + 1) * C : (2 * b + 2) * C, at] = (t * ga[:, at]).astype(BF16)
            return 0

        lax.fori_loop(0, ROWS // 2, project_grad, 0)
        wg[2 * b * C : (2 * b + 2) * C, :] = dot_nt(gpt[2 * b * C : (2 * b + 2) * C, :], xbf[...])

    def copy1(t):
        other, device = xy_peer(t)
        return remote(wg.at[pl.ds(pl.multiple_of(other * 48, 48), 48), :], part1.at[my_xy], s_w.at[0, t], r_w.at[0, t], device)

    def copy2(t):
        other, device = zc_peer(t)
        return remote(piece.at[other], part2.at[my_zc], s_w.at[1, t], r_w.at[1, t], device)

    def copy3(t):
        other, device = zc_peer(t)
        return remote(mine, part3.at[my_zc], s_w.at[2, t], r_w.at[2, t], device)

    def copy4(t):
        other, device = xy_peer(t)
        return remote(stage.at[pl.ds(0, 48), :], part4.at[my_xy], s_w.at[3, t], r_w.at[3, t], device)

    def each(copy, what):
        def one(t, _):
            getattr(copy(t), what)()
            return 0

        lax.fori_loop(1, 16, one, 0)

    each(copy1, "start")
    part1[my_xy] = wg[pl.ds(pl.multiple_of(my_xy * 48, 48), 48), :]

    def pair_grad(n, _):
        at = lanes(n, 2 * N)
        dx = dot(win[...], gpt[:, at])
        xh = xhat[:, at]
        gx = scin[:, at] * (dx - mean0(dx) - xh * mean0(dx * xh))
        for q in range(2):
            gpair[2 * n + q] = gx[:, q * N : (q + 1) * N].T.astype(BF16)
        return 0

    lax.fori_loop(0, ROWS // 2, pair_grad, 0)

    each(copy1, "wait_recv")
    total = part1[0]
    for t in range(1, 16):
        total = total + part1[t]
    for t in range(16):
        piece[t] = total[3 * t : 3 * t + 3, :]
    each(copy2, "start")
    part2[my_zc] = piece[my_zc]
    each(copy2, "wait_recv")
    total = part2[0]
    for t in range(1, 16):
        total = total + part2[t]
    mine[...] = total
    each(copy3, "start")
    part3[my_zc] = total
    each(copy3, "wait_recv")
    for t in range(16):
        stage[3 * t : 3 * t + 3, :] = part3[t]
    each(copy4, "start")
    part4[my_xy] = stage[:48, :]
    each(copy4, "wait_recv")

    whole = part4[...].reshape(6 * C, C)
    squares = jnp.sum(jnp.sum(whole * whole, axis=0, keepdims=True), axis=1, keepdims=True)
    clip = jnp.minimum(1.0, lax.rsqrt(squares * (1.0 / (6 * C * C)) + 1e-06))
    for b in range(5):
        gwin[:, b * C : (b + 1) * C] = whole[b * C : (b + 1) * C].T * clip
    gwout[...] = whole[5 * C :] * clip

    def sent(step, _):
        for cp in copy_lr(step):
            cp.wait_send()
        copy_g(step).wait_send()
        for g in range(NG):
            copy_back(tri, tri_r, s_t, r_t, g, step).wait_send()
            copy_back(gl, gl_r, s_gl, r_gl, g, step).wait_send()
            copy_back(gr, gr_r, s_gr, r_gr, g, step).wait_send()
        return 0

    lax.fori_loop(0, PEERS, sent, 0)
    for copy in (copy1, copy2, copy3, copy4):
        each(copy, "wait_send")


def body(pair, pair_mask, cotangent, w_in, w_out):
    v = pltpu.VMEM
    dma = pltpu.SemaphoreType.DMA
    wide = v((C, WIDE), F32)
    wide_bf = v((C, WIDE), BF16)
    chan = v((CH, N, N), BF16)
    rows = v((C, ROWS, N), BF16)
    blocks = v((8, CH, ROWS, N), BF16)
    scratch = [
        v((8, 4 * CH, C), BF16), v((C, C), BF16), v((C, C), BF16),
        wide, wide_bf, v((1, WIDE), F32),
        v((CH * ROWS, N), F32), v((CH * ROWS, N), F32),
        blocks, blocks, chan, chan,
        wide, wide, wide, wide,
        wide, wide, wide_bf, wide, wide_bf, v((5 * C, WIDE), BF16),
        chan, rows, blocks, chan, v((C * ROWS, N), F32),
        chan, chan, rows, rows,
        v((6 * C, C), F32), v((16, 48, C), F32), v((16, 3, C), F32), v((16, 3, C), F32), v((3, C), F32), v((16, 3, C), F32),
        v((C * ROWS, N), F32), v((16, 48, C), F32),
        dma((PEERS,)), dma((PEERS,)), dma((PEERS,)), dma((PEERS,)),
        dma((PEERS, NG)), dma((PEERS, NG)), dma((PEERS,)), dma((PEERS,)),
        dma((PEERS, NG)), dma((PEERS, NG)), dma((PEERS, NG)), dma((PEERS, NG)),
        dma((4, 16)), dma((4, 16)),
    ]
    vm = pl.BlockSpec(memory_space=pltpu.VMEM)
    update, grad_pair, grad_win, grad_wout = pl.pallas_call(
        kernel,
        name="triangle",
        out_shape=(
            jax.ShapeDtypeStruct((ROWS, N, C), BF16),
            jax.ShapeDtypeStruct((ROWS, N, C), BF16),
            jax.ShapeDtypeStruct((C, 5 * C), F32),
            jax.ShapeDtypeStruct((C, C), F32),
        ),
        in_specs=[vm] * 5,
        out_specs=(vm,) * 4,
        scratch_shapes=scratch,
        compiler_params=pltpu.CompilerParams(collective_id=0, has_side_effects=True, vmem_limit_bytes=56 * 2**20),
    )(pair[0], pair_mask[0], cotangent[0], w_in, w_out)
    return update[None], grad_pair[None], grad_win, grad_wout


def solution(mesh):
    in_specs = (P("dp", "dap", None, None), P("dp", "dap", None), P("dp", "dap", None, None), P(), P())
    out_specs = (P("dp", "dap", None, None), P("dp", "dap", None, None), P(), P())
    return jax.shard_map(body, mesh=mesh, in_specs=in_specs, out_specs=out_specs, check_vma=False)
```

```python
import functools

import jax
import jax.numpy as jnp
from jax import lax
from jax.experimental import pallas as pl
from jax.experimental.pallas import tpu as pltpu
from jax.sharding import PartitionSpec as P

EPS = 1e-05
MESH = pl.DeviceIdType.MESH
F32 = jnp.float32
BF16 = jnp.bfloat16

C = 128
N = 128
ROWS = 16
CH = 32
HALF = N // 2
WIDE = ROWS * N
GROUP = 8
NG = CH // GROUP
PEERS = 7
XP = 3
XY = sorted(
    ((dx, dy) for dx in range(4) for dy in range(4) if dx or dy),
    key=lambda d: (-min(d[0], 4 - d[0]) - min(d[1], 4 - d[1]), d),
)
ZS = (4, 3, 5, 2, 6, 1, 7)


def dot(a, b):
    return lax.dot_general(a, b, (((1,), (0,)), ((), ())), preferred_element_type=F32)


def dot_nt(a, b):
    return lax.dot_general(a, b, (((1,), (1,)), ((), ())), preferred_element_type=F32)


def dot_tn(a, b):
    return lax.dot_general(a, b, (((0,), (0,)), ((), ())), preferred_element_type=F32)


def sigmoid(v):
    return 1.0 / (1.0 + jnp.exp(-v))


def mean0(v):
    return jnp.sum(v, axis=0, keepdims=True) * (1.0 / C)


def lanes(chunk, width):
    return pl.ds(pl.multiple_of(chunk * width, width), width)


def remote(src, dst, send_sem, recv_sem, device):
    return pltpu.make_async_remote_copy(
        src_ref=src, dst_ref=dst, send_sem=send_sem, recv_sem=recv_sem, device_id=device, device_id_type=MESH
    )


def kernel(
    pair, mask, cot_hbm, win, wout, upd_hbm, gpair_hbm, sums, cot, upd, gpair,
    wt4, wog, woutt, xhat, xbf, scin, stage, send_l, send_r, recv_l, recv_r,
    al, bl, ar, br, ogs, a2, got, dt, tbt, gpt,
    tri, tri_r, send_g, recv_g, grad, gl, gr, gl_r, gr_r, early, late, half,
    e_core, e_half, e_xy, e_sum, e_z, l_core, l_half, l_xy, l_sum, l_z,
    s_l, r_l, s_r, r_r, s_t, r_t, s_g, r_g, s_gl, r_gl, s_gr, r_gr, s_w, r_w, io,
):
    cot_in = pltpu.make_async_copy(cot_hbm, cot, io.at[0])
    cot_in.start()
    dp, me = lax.axis_index("dp"), lax.axis_index("dap")
    zh, x = me // 4, me % 4
    y, zlo, core = dp // 8, (dp // 2) % 4, dp % 2

    z = zh * 4 + zlo

    def row_peer(k):
        return ((zh + 1 - k // 4) % 2) * 4 + x_peer(k)

    def x_peer(k):
        return (x + k + 2 + k // 6) % 4

    def place(px, py, pz, pcore):
        return (py * 4 + pz % 4) * 2 + pcore, (pz // 4) * 4 + px

    def xy_peer(t):
        dx, dy = XY[t]
        px, py = (x + dx) % 4, (y + dy) % 4
        return py * 4 + px, place(px, py, z, core)

    def z_peer(t):
        return place(x, y, (z + ZS[t]) % 8, core)

    other_core = place(x, y, z, 1 - core)
    my_xy = y * 4 + x

    barrier = pltpu.get_barrier_semaphore()
    greet = [xy_peer(t)[1] for t in range(15)] + [z_peer(t) for t in range(7)] + [other_core]
    greet += [(dp, row_peer(step)) for step in (0, 1, 3)]
    for device in greet:
        pl.semaphore_signal(barrier, inc=1, device_id=device, device_id_type=MESH)

    for b in range(5):
        block = win[:, b * C : (b + 1) * C].astype(F32).T.astype(BF16)
        if b == 4:
            wog[...] = block
        else:
            for e in range(4):
                wt4[b // 2, e, (b % 2) * CH : (b % 2 + 1) * CH, :] = block[e * CH : (e + 1) * CH, :]
    woutt[...] = wout[...].astype(F32).T.astype(BF16)

    def norm_pair(i, _):
        v = pair[i].astype(F32).T
        cen = v - mean0(v)
        sc = lax.rsqrt(mean0(cen * cen) + EPS)
        xh = cen * sc
        at = lanes(i, N)
        xhat[:, at] = xh
        xbf[:, at] = xh.astype(BF16)
        scin[:, at] = sc
        return 0

    lax.fori_loop(0, ROWS, norm_pair, 0, unroll=2)

    def project(side, e):
        ga, gb = ((al, bl), (ar, br))[side]
        rows = pl.ds(pl.multiple_of(e * CH, CH), CH)
        for n in range(4):
            at = slice(n * 4 * N, (n + 1) * 4 * N)
            p = dot(wt4[side, e], xbf[:, at])
            m = jnp.concatenate([mask[4 * n + q : 4 * n + q + 1, :] for q in range(4)], axis=1).astype(F32)
            s = sigmoid(p[:CH])
            sm = s * m
            v = sm * p[CH:]
            ga[rows, at] = sm
            gb[rows, at] = v * (1.0 - s)
            for q in range(4):
                stage[pl.ds(4 * n + q, CH, stride=ROWS), :] = v[:, q * N : (q + 1) * N]
        return stage[...].astype(BF16).reshape(CH, ROWS, N)

    my_rows = pl.ds(pl.multiple_of(me * ROWS, ROWS), ROWS)
    my_half_rows = pl.ds(pl.multiple_of(x * ROWS, ROWS), ROWS)
    my_ch = pl.multiple_of(x * CH, CH)

    def copy_r(k):
        return remote(send_r.at[x_peer(k)], recv_r.at[:, my_rows, :], s_r.at[k], r_r.at[k], (dp, row_peer(k)))

    def copy_l(t):
        e = x_peer(4 + t)
        return remote(send_l.at[e], recv_l.at[:, my_half_rows, :], s_l.at[t], r_l.at[t], (dp, row_peer(4 + t)))

    def send_right(t, _):
        e = x_peer(4 + t)
        send_r[e] = project(1, e)
        copy_r(t + t // 2).start()
        copy_r(4 + t).start()
        return 0

    def send_left(t, _):
        e = x_peer(4 + t)
        send_l[e] = project(0, e)
        copy_l(t).start()
        return 0

    pl.semaphore_wait(barrier, 26)
    lax.fori_loop(0, XP, send_right, 0)
    own = project(1, x)
    send_r[x] = own
    copy_r(2).start()
    recv_r[:, my_rows, :] = own
    lax.fori_loop(0, XP, send_left, 0)
    recv_l[:, my_half_rows, :] = project(0, x)

    def gate(n, _):
        at = lanes(n, 2 * N)
        og = sigmoid(dot(wog[...], xbf[:, at]))
        g = jnp.concatenate([cot[2 * n].astype(F32).T, cot[2 * n + 1].astype(F32).T], axis=1)
        go = g * og
        gob = go.astype(BF16)
        ogs[:, at] = og
        a2[:, at] = go * (1.0 - og)
        got[:, at] = gob
        dt[:, at] = dot(wout[...], gob)
        return 0

    cot_in.wait()
    lax.fori_loop(0, ROWS // 2, gate, 0)

    def wait_recv(copy, count):
        def one(t, _):
            copy(t).wait_recv()
            return 0

        lax.fori_loop(0, count, one, 0)

    def wait_send(copy, count):
        def one(t, _):
            copy(t).wait_send()
            return 0

        lax.fori_loop(0, count, one, 0)

    wait_recv(copy_l, XP)
    wait_recv(copy_r, PEERS)

    def exchange(make, src, dst, ss, rs, first):
        def copy(t):
            g, k = t // (PEERS - first), first + t % (PEERS - first)
            e = row_peer(k) if first == 0 else x_peer(k)
            cs = pl.multiple_of(g * GROUP, GROUP)
            return remote(
                src.at[pl.ds(cs, GROUP), pl.ds(pl.multiple_of(e * ROWS, ROWS), ROWS), :],
                dst.at[pl.ds(my_ch + cs, GROUP), :, :],
                ss.at[t], rs.at[t], (dp, row_peer(k)),
            )

        def group(g, _):
            for q in range(GROUP):
                c = g * GROUP + q
                src[c] = make(c).astype(BF16)
            cs = pl.multiple_of(g * GROUP, GROUP)

            def start(t, _):
                copy(g * (PEERS - first) + t).start()
                return 0

            lax.fori_loop(0, PEERS - first, start, 0)
            dst[pl.ds(my_ch + cs, GROUP)] = src[pl.ds(cs, GROUP), my_rows if first == 0 else my_half_rows, :]
            return 0

        lax.fori_loop(0, NG, group, 0)
        return copy

    def widen(*parts):
        def part(t, _):
            at = pl.ds(pl.multiple_of(t * 8, 8), 8)
            total = parts[0][at].astype(F32)
            for more in parts[1:]:
                total = total + more[at].astype(F32)
            half[pl.ds(pl.multiple_of(t * N, N), N), :] = total.reshape(N, N)
            return 0

        lax.fori_loop(0, ROWS, part, 0, unroll=2)

    copy_t = exchange(lambda c: dot_nt(recv_l[c], recv_r[c]), tri, tri_r, s_t, r_t, 4)
    wait_recv(copy_t, XP * NG)
    widen(tri_r)

    def rows_step(n, _):
        at = lanes(n, 2 * N)
        t = jnp.concatenate([half[pl.ds(2 * n + q, C, stride=ROWS), :] for q in range(2)], axis=1)
        cen = t - mean0(t)
        sc = lax.rsqrt(mean0(cen * cen) + EPS)
        tn = cen * sc
        tb = tn.astype(BF16)
        tbt[:, at] = tb
        out = dot(woutt[...], tb)
        u = ogs[:, at] * out
        gpt[4 * C :, at] = (a2[:, at] * out).astype(BF16)
        d = dt[:, at]
        gt = sc * (d - mean0(d) - tn * mean0(d * tn))
        for q in range(2):
            upd[2 * n + q] = u[:, q * N : (q + 1) * N].T.astype(BF16)
            grad[pl.ds(2 * n + q, C, stride=ROWS), :] = gt[:, q * N : (q + 1) * N]
        return 0

    lax.fori_loop(0, ROWS // 2, rows_step, 0)
    upd_out = pltpu.make_async_copy(upd, upd_hbm, io.at[1])
    upd_out.start()

    def copy_g(t):
        e = x_peer(4 + t)
        return remote(send_g.at[e], recv_g.at[:, my_half_rows, :], s_g.at[t], r_g.at[t], (dp, row_peer(4 + t)))

    def narrow(e):
        rows = pl.ds(pl.multiple_of(e * CH * ROWS, CH * ROWS), CH * ROWS)
        return grad[rows, :].astype(BF16).reshape(CH, ROWS, N)

    def start_g(t, _):
        e = x_peer(4 + t)
        send_g[e] = narrow(e)
        copy_g(t).start()
        return 0

    lax.fori_loop(0, XP, start_g, 0)
    recv_g[:, my_half_rows, :] = narrow(x)

    early[3 * C :, :] = dot_nt(tbt[...], got[...])
    early[2 * C : 3 * C, :] = dot_nt(gpt[4 * C :, :], xbf[...])

    wait_recv(copy_g, XP)
    copy_gr = exchange(lambda c: dot_tn(recv_g[c], recv_l[c]), gr, gr_r.at[zh], s_gr, r_gr, 0)
    copy_gl = exchange(lambda c: dot(recv_g[c], recv_r[c]), gl, gl_r, s_gl, r_gl, 4)

    def side_grad(b, ga, gb, out, *parts):
        widen(*parts)

        def project_grad(n, _):
            at = lanes(n, 2 * N)
            t = jnp.concatenate([half[pl.ds(2 * n + q, C, stride=ROWS), :] for q in range(2)], axis=1)
            gpt[2 * b * C : (2 * b + 1) * C, at] = (t * gb[:, at]).astype(BF16)
            gpt[(2 * b + 1) * C : (2 * b + 2) * C, at] = (t * ga[:, at]).astype(BF16)
            return 0

        lax.fori_loop(0, ROWS // 2, project_grad, 0)
        out[: 2 * C, :] = dot_nt(gpt[2 * b * C : (2 * b + 2) * C, :], xbf[...])

    def reduction(at, own, base, from_core, halves, from_xy, chunk, from_z):
        n = own.shape[0] // 2
        m = n // 16
        mine = pl.ds(pl.multiple_of(core * n, n), n)
        theirs = pl.ds(pl.multiple_of((1 - core) * n, n), n)
        final = sums.at[pl.ds(pl.multiple_of(base + core * n, n), n), :]

        def sem(k):
            return s_w.at[at, k], r_w.at[at, k]

        def scatter_core():
            return [remote(own.at[theirs, :], from_core, *sem(0), other_core)]

        def scatter_xy():
            copies = []
            for t in range(15):
                other, device = xy_peer(t)
                copies.append(remote(halves.at[pl.ds(pl.multiple_of(other * m, m), m), :], from_xy.at[my_xy], *sem(1 + t), device))
            return copies

        def exchange_z():
            return [remote(chunk.at[0], from_z.at[z], *sem(16 + t), z_peer(t)) for t in range(7)]

        def gather_xy():
            place_at = sums.at[pl.ds(pl.multiple_of(base + core * n + my_xy * m, m), m), :]
            return [remote(chunk.at[1], place_at, *sem(23 + t), xy_peer(t)[1]) for t in range(15)]

        def gather_core():
            return [remote(final, final, *sem(38), other_core)]

        steps = [scatter_core, scatter_xy, exchange_z, gather_xy, gather_core]

        def go(k):
            if k:
                for copy in steps[k - 1]():
                    copy.wait_recv()
            if k == 1:
                halves[...] = own[mine, :] + from_core[...]
                from_xy[my_xy] = halves[pl.ds(pl.multiple_of(my_xy * m, m), m), :]
            if k == 2:
                total = from_xy[0]
                for t in range(1, 16):
                    total = total + from_xy[t]
                chunk[0] = total
                from_z[z] = total
            if k == 3:
                total = from_z[0]
                for t in range(1, 8):
                    total = total + from_z[t]
                chunk[1] = total
                sums[pl.ds(pl.multiple_of(base + core * n + my_xy * m, m), m), :] = total
            if k < 5:
                for copy in steps[k]():
                    copy.start()

        def sent():
            for step in steps:
                for copy in step():
                    copy.wait_send()

        return go, sent

    def pair_grad(n, _):
        at = lanes(n, 2 * N)
        dx = dot(win[...], gpt[:, at])
        xh = xhat[:, at]
        gx = scin[:, at] * (dx - mean0(dx) - xh * mean0(dx * xh))
        for q in range(2):
            gpair[2 * n + q] = gx[:, q * N : (q + 1) * N].T.astype(BF16)
        return 0

    go_early, sent_early = reduction(0, early, 0, e_core, e_half, e_xy, e_sum, e_z)
    go_late, sent_late = reduction(1, late, 4 * C, l_core, l_half, l_xy, l_sum, l_z)

    wait_recv(copy_gl, XP * NG)
    side_grad(0, al, bl, early, gl_r)
    go_early(0)
    go_early(1)
    wait_recv(copy_gr, PEERS * NG)
    side_grad(1, ar, br, late, gr_r.at[0], gr_r.at[1])
    go_late(0)
    go_early(2)
    go_late(1)
    lax.fori_loop(0, ROWS // 4, pair_grad, 0)
    go_early(3)
    go_late(2)
    lax.fori_loop(ROWS // 4, ROWS // 2, pair_grad, 0)
    gpair_out = pltpu.make_async_copy(gpair, gpair_hbm, io.at[2])
    gpair_out.start()
    go_early(4)
    go_late(3)
    go_late(4)
    go_early(5)
    go_late(5)

    for copy, count in ((copy_l, XP), (copy_r, PEERS), (copy_t, XP * NG), (copy_g, XP), (copy_gl, XP * NG), (copy_gr, PEERS * NG)):
        wait_send(copy, count)
    sent_early()
    sent_late()
    upd_out.wait()
    gpair_out.wait()


def finish(upd_in, gpair_in, sums, upd, gpair, gwin, gwout):
    upd[...] = upd_in[...]
    gpair[...] = gpair_in[...]
    whole = sums[...]
    squares = jnp.sum(jnp.sum(whole * whole, axis=0, keepdims=True), axis=1, keepdims=True)
    clip = jnp.minimum(1.0, lax.rsqrt(squares * (1.0 / (6 * C * C)) + 1e-06))
    for b, at in enumerate((0, 1, 4, 5, 2)):
        gwin[:, b * C : (b + 1) * C] = whole[at * C : (at + 1) * C].T * clip
    gwout[...] = whole[3 * C : 4 * C] * clip


def body(pair, pair_mask, cotangent, w_in, w_out):
    v = pltpu.VMEM
    dma = pltpu.SemaphoreType.DMA
    wide = v((C, WIDE), F32)
    wide_bf = v((C, WIDE), BF16)
    chan_half = v((CH, HALF, N), BF16)
    chan = v((CH, N, N), BF16)
    rows = v((C, ROWS, N), BF16)
    own = v((ROWS, N, C), BF16)
    blocks = v((4, CH, ROWS, N), BF16)

    def reduction(n):
        return [v((n // 2, C), F32), v((n // 2, C), F32), v((16, n // 32, C), F32), v((2, n // 32, C), F32), v((8, n // 32, C), F32)]

    scratch = [
        own, own, own,
        v((2, 4, 2 * CH, C), BF16), v((C, C), BF16), v((C, C), BF16),
        wide, wide_bf, v((1, WIDE), F32),
        v((CH * ROWS, N), F32),
        blocks, blocks, chan_half, chan,
        wide, wide, wide, wide,
        wide, wide, wide_bf, wide, wide_bf, v((5 * C, WIDE), BF16),
        chan_half, rows, blocks, chan_half, v((C * ROWS, N), F32),
        chan_half, chan, rows, v((2, C, ROWS, N), BF16),
        v((4 * C, C), F32), v((2 * C, C), F32), v((C * ROWS, N), F32),
        *reduction(4 * C), *reduction(2 * C),
        dma((XP,)), dma((XP,)), dma((PEERS,)), dma((PEERS,)),
        dma((XP * NG,)), dma((XP * NG,)), dma((XP,)), dma((XP,)),
        dma((XP * NG,)), dma((XP * NG,)), dma((PEERS * NG,)), dma((PEERS * NG,)),
        dma((2, 39)), dma((2, 39)), dma((3,)),
    ]
    vm = pl.BlockSpec(memory_space=pltpu.VMEM)
    hbm = pl.BlockSpec(memory_space=pl.ANY)
    edges = jax.ShapeDtypeStruct((ROWS, N, C), BF16)
    update, grad_pair, sums = pl.pallas_call(
        kernel,
        name="triangle",
        out_shape=(edges, edges, jax.ShapeDtypeStruct((6 * C, C), F32)),
        in_specs=[vm, vm, hbm, vm, vm],
        out_specs=(hbm, hbm, vm),
        scratch_shapes=scratch,
        compiler_params=pltpu.CompilerParams(collective_id=0, has_side_effects=True, vmem_limit_bytes=56 * 2**20),
    )(pair[0], pair_mask[0], cotangent[0], w_in, w_out)
    update, grad_pair, grad_win, grad_wout = pl.pallas_call(
        finish,
        name="finish",
        out_shape=(edges, edges, jax.ShapeDtypeStruct((C, 5 * C), F32), jax.ShapeDtypeStruct((C, C), F32)),
        in_specs=[vm] * 3,
        out_specs=(vm,) * 4,
    )(update, grad_pair, sums)
    return update[None], grad_pair[None], grad_win, grad_wout


def solution(mesh):
    in_specs = (P("dp", "dap", None, None), P("dp", "dap", None), P("dp", "dap", None, None), P(), P())
    out_specs = (P("dp", "dap", None, None), P("dp", "dap", None, None), P(), P())
    return jax.shard_map(body, mesh=mesh, in_specs=in_specs, out_specs=out_specs, check_vma=False)
```

```python
import functools

import jax
import jax.numpy as jnp
from jax import lax
from jax.experimental import pallas as pl
from jax.experimental.pallas import tpu as pltpu
from jax.sharding import PartitionSpec as P

EPS = 1e-05
MESH = pl.DeviceIdType.MESH
F32 = jnp.float32
BF16 = jnp.bfloat16

C = 128
N = 128
ROWS = 16
CH = 32
HALF = N // 2
WIDE = ROWS * N
GROUP = 8
NG = CH // GROUP
XP = 3
XY = sorted(
    ((dx, dy) for dx in range(4) for dy in range(4) if dx or dy),
    key=lambda d: (-min(d[0], 4 - d[0]) - min(d[1], 4 - d[1]), d),
)
ZS = (4, 3, 5, 2, 6, 1, 7)


def dot(a, b):
    return lax.dot_general(a, b, (((1,), (0,)), ((), ())), preferred_element_type=F32)


def dot_nt(a, b):
    return lax.dot_general(a, b, (((1,), (1,)), ((), ())), preferred_element_type=F32)


def dot_tn(a, b):
    return lax.dot_general(a, b, (((0,), (0,)), ((), ())), preferred_element_type=F32)


def sigmoid(v):
    return 1.0 / (1.0 + jnp.exp(-v))


def mean0(v):
    return jnp.sum(v, axis=0, keepdims=True) * (1.0 / C)


def lanes(chunk, width):
    return pl.ds(pl.multiple_of(chunk * width, width), width)


def remote(src, dst, send_sem, recv_sem, device):
    return pltpu.make_async_remote_copy(
        src_ref=src, dst_ref=dst, send_sem=send_sem, recv_sem=recv_sem, device_id=device, device_id_type=MESH
    )


def kernel(
    pair_own, mask_own, cot_own, win_hbm, wout_hbm, upd_hbm, gpair_hbm, sums, pair, mask, cot, win, wout, upd, gpair,
    wt4, wog, woutt, xhat, xbf, scin, stage, send_l, send_r, recv_l, recv_r,
    al, bl, ar, br, ogs, a2, got, dt, tbt, gpt,
    tri, tri_r, send_g, recv_g, grad, gl, gr, gr_own, gr_out, gr_in, gl_r, gr_r, early, late, half,
    e_core, e_half, e_xy, e_sum, e_z, l_core, l_half, l_xy, l_sum, l_z,
    s_l, r_l, s_r, r_r, s_rc, r_rc, s_t, r_t, s_g, r_g, s_gl, r_gl, s_gr, r_gr, s_gc, r_gc, s_w, r_w, s_in, r_in, s_out, r_out, io,
):
    dp, me = lax.axis_index("dp"), lax.axis_index("dap")
    zh, x = me // 4, me % 4
    y, zlo, core = dp // 8, (dp // 2) % 4, dp % 2

    z = zh * 4 + zlo

    swapped = core != zh

    def x_peer(t):
        return (x + 2 + t + t // 2) % 4

    def place(px, py, pz, pcore):
        return (py * 4 + pz % 4) * 2 + pcore, (pz // 4) * 4 + px

    def xy_peer(t):
        dx, dy = XY[t]
        px, py = (x + dx) % 4, (y + dy) % 4
        return py * 4 + px, place(px, py, z, core)

    def z_peer(t):
        return place(x, y, (z + ZS[t]) % 8, core)

    other_core = place(x, y, z, 1 - core)
    partner = place(x, y, (z + 4) % 8, 1 - core)

    def x_device(t):
        return place(x_peer(t), y, z, core)

    my_xy = y * 4 + x

    barrier = pltpu.get_barrier_semaphore()
    greet = [xy_peer(t)[1] for t in range(15)] + [z_peer(t) for t in range(7)] + [other_core]
    greet += [partner]
    for device in greet:
        pl.semaphore_signal(barrier, inc=1, device_id=device, device_id_type=MESH)

    def swap_in(n):
        if n < 4:
            src, dst = pair_own.at[pl.ds(4 * n, 4)], pair.at[pl.ds(4 * n, 4)]
        else:
            src, dst = ((mask_own, mask), (cot_own, cot))[n - 4]
        return remote(src, dst, s_in.at[n], r_in.at[n], partner)

    def keep_in(n):
        src, dst = ((pair_own, pair), (mask_own, mask), (cot_own, cot))[n]
        return pltpu.make_async_copy(src, dst, io.at[n])

    weights = [pltpu.make_async_copy(win_hbm, win, io.at[3]), pltpu.make_async_copy(wout_hbm, wout, io.at[4])]
    for copy in weights:
        copy.start()

    @pl.when(jnp.logical_not(swapped))
    def _():
        for n in range(3):
            keep_in(n).start()

    for copy in weights:
        copy.wait()
    for b in range(5):
        block = win[:, b * C : (b + 1) * C].astype(F32).T.astype(BF16)
        if b == 4:
            wog[...] = block
        else:
            for e in range(4):
                wt4[b // 2, e, (b % 2) * CH : (b % 2 + 1) * CH, :] = block[e * CH : (e + 1) * CH, :]
    woutt[...] = wout[...].astype(F32).T.astype(BF16)

    pl.semaphore_wait(barrier, 24)

    @pl.when(swapped)
    def _():
        for n in (4, 0, 1, 2, 3):
            swap_in(n).start()

    @pl.when(jnp.logical_not(swapped))
    def _():
        for n in range(3):
            keep_in(n).wait()


    def norm_pair(i, _):
        v = pair[i].astype(F32).T
        cen = v - mean0(v)
        sc = lax.rsqrt(mean0(cen * cen) + EPS)
        xh = cen * sc
        at = lanes(i, N)
        xhat[:, at] = xh
        xbf[:, at] = xh.astype(BF16)
        scin[:, at] = sc
        return 0

    def project(n):
        at = lanes(n, 4 * N)
        m = jnp.concatenate([mask[pl.ds(4 * n + q, 1), :] for q in range(4)], axis=1).astype(F32)
        for side, (ga, gb) in enumerate(((al, bl), (ar, br))):
            for e in range(4):
                rows = slice(e * CH, (e + 1) * CH)
                p = dot(wt4[side, e], xbf[:, at])
                s = sigmoid(p[:CH])
                sm = s * m
                v = sm * p[CH:]
                ga[rows, at] = sm
                gb[rows, at] = v * (1.0 - s)
                for q in range(4):
                    stage[side, e, pl.ds(4 * n + q, CH, stride=ROWS), :] = v[:, q * N : (q + 1) * N]

    for n in range(4):
        @pl.when(swapped)
        def _():
            if n == 0:
                swap_in(4).wait_recv()
            swap_in(n).wait_recv()
            if n == 3:
                swap_in(5).start()

        lax.fori_loop(4 * n, 4 * n + 4, norm_pair, 0, unroll=2)
        project(n)

    my_half = pl.ds(pl.multiple_of(core * HALF, HALF), HALF)
    my_rows = pl.ds(pl.multiple_of(core * HALF + x * ROWS, ROWS), ROWS)
    my_half_rows = pl.ds(pl.multiple_of(x * ROWS, ROWS), ROWS)
    my_ch = pl.multiple_of(x * CH, CH)

    def rounded(side, e):
        return stage[side, e].astype(BF16).reshape(CH, ROWS, N)

    def copy_r(t):
        return remote(send_r.at[x_peer(t)], recv_r.at[:, my_rows, :], s_r.at[t], r_r.at[t], x_device(t))

    def copy_l(t):
        return remote(send_l.at[x_peer(t)], recv_l.at[:, my_half_rows, :], s_l.at[t], r_l.at[t], x_device(t))

    def copy_rc(t):
        at = pl.ds(pl.multiple_of(t * GROUP, GROUP), GROUP)
        return remote(recv_r.at[at, my_half, :], recv_r.at[at, my_half, :], s_rc.at[t], r_rc.at[t], other_core)

    def send_right(t, _):
        e = x_peer(t)
        send_r[e] = rounded(1, e)
        copy_r(t).start()
        return 0

    def send_left(t, _):
        e = x_peer(t)
        send_l[e] = rounded(0, e)
        copy_l(t).start()
        return 0

    lax.fori_loop(0, XP, send_right, 0)
    lax.fori_loop(0, XP, send_left, 0)
    recv_r[:, my_rows, :] = rounded(1, x)
    recv_l[:, my_half_rows, :] = rounded(0, x)

    def gate(n, _):
        at = lanes(n, 2 * N)
        ogs[:, at] = sigmoid(dot(wog[...], xbf[:, at]))
        return 0

    lax.fori_loop(0, ROWS // 2, gate, 0)

    def gate_cot(n, _):
        at = lanes(n, 2 * N)
        og = ogs[:, at]
        g = jnp.concatenate([cot[2 * n].astype(F32).T, cot[2 * n + 1].astype(F32).T], axis=1)
        go = g * og
        gob = go.astype(BF16)
        a2[:, at] = go * (1.0 - og)
        got[:, at] = gob
        dt[:, at] = dot(wout[...], gob)
        return 0

    def wait_recv(copy, count):
        def one(t, _):
            copy(t).wait_recv()
            return 0

        lax.fori_loop(0, count, one, 0)

    def wait_send(copy, count):
        def one(t, _):
            copy(t).wait_send()
            return 0

        lax.fori_loop(0, count, one, 0)

    wait_recv(copy_r, XP)
    for t in range(NG):
        copy_rc(t).start()
    wait_recv(copy_l, XP)
    wait_recv(copy_rc, NG)

    def exchange(make, src, dst, ss, rs):
        def copy(t):
            g, k = t // XP, t % XP
            cs = pl.multiple_of(g * GROUP, GROUP)
            return remote(
                src.at[pl.ds(cs, GROUP), pl.ds(pl.multiple_of(x_peer(k) * ROWS, ROWS), ROWS), :],
                dst.at[pl.ds(my_ch + cs, GROUP), :, :],
                ss.at[t], rs.at[t], x_device(k),
            )

        def group(g, _):
            for q in range(GROUP):
                c = g * GROUP + q
                src[c] = make(c).astype(BF16)
            cs = pl.multiple_of(g * GROUP, GROUP)

            def start(t, _):
                copy(g * XP + t).start()
                return 0

            lax.fori_loop(0, XP, start, 0)
            dst[pl.ds(my_ch + cs, GROUP)] = src[pl.ds(cs, GROUP), my_half_rows, :]
            return 0

        lax.fori_loop(0, NG, group, 0)
        return copy

    def widen(src):
        def part(t, _):
            at = pl.ds(pl.multiple_of(t * 8, 8), 8)
            half[pl.ds(pl.multiple_of(t * N, N), N), :] = src[at].astype(F32).reshape(N, N)
            return 0

        lax.fori_loop(0, ROWS, part, 0, unroll=2)

    copy_t = exchange(lambda c: dot_nt(recv_l[c], recv_r[c]), tri, tri_r, s_t, r_t)

    @pl.when(swapped)
    def _():
        swap_in(5).wait_recv()

    lax.fori_loop(0, ROWS // 2, gate_cot, 0)
    wait_recv(copy_t, XP * NG)
    widen(tri_r)

    def rows_step(n, _):
        at = lanes(n, 2 * N)
        t = jnp.concatenate([half[pl.ds(2 * n + q, C, stride=ROWS), :] for q in range(2)], axis=1)
        cen = t - mean0(t)
        sc = lax.rsqrt(mean0(cen * cen) + EPS)
        tn = cen * sc
        tb = tn.astype(BF16)
        tbt[:, at] = tb
        out = dot(woutt[...], tb)
        u = ogs[:, at] * out
        gpt[4 * C :, at] = (a2[:, at] * out).astype(BF16)
        d = dt[:, at]
        gt = sc * (d - mean0(d) - tn * mean0(d * tn))
        for q in range(2):
            upd[2 * n + q] = u[:, q * N : (q + 1) * N].T.astype(BF16)
            grad[pl.ds(2 * n + q, C, stride=ROWS), :] = gt[:, q * N : (q + 1) * N]
        return 0

    lax.fori_loop(0, ROWS // 2, rows_step, 0)

    def swap_out(n):
        if n == 0:
            src, dst = upd, upd_hbm
        else:
            src, dst = gpair.at[pl.ds(4 * (n - 1), 4)], gpair_hbm.at[pl.ds(4 * (n - 1), 4)]
        return remote(src, dst, s_out.at[n], r_out.at[n], partner), pltpu.make_async_copy(src, dst, io.at[5 + n])

    def send_out(n):
        @pl.when(swapped)
        def _():
            swap_out(n)[0].start()

        @pl.when(jnp.logical_not(swapped))
        def _():
            swap_out(n)[1].start()

    send_out(0)

    def copy_g(t):
        return remote(send_g.at[x_peer(t)], recv_g.at[:, my_half_rows, :], s_g.at[t], r_g.at[t], x_device(t))

    def narrow(e):
        rows = pl.ds(pl.multiple_of(e * CH * ROWS, CH * ROWS), CH * ROWS)
        return grad[rows, :].astype(BF16).reshape(CH, ROWS, N)

    def start_g(t, _):
        e = x_peer(t)
        send_g[e] = narrow(e)
        copy_g(t).start()
        return 0

    lax.fori_loop(0, XP, start_g, 0)
    recv_g[:, my_half_rows, :] = narrow(x)

    early[3 * C :, :] = dot_nt(tbt[...], got[...])
    early[2 * C : 3 * C, :] = dot_nt(gpt[4 * C :, :], xbf[...])

    wait_recv(copy_g, XP)
    copy_gl = exchange(lambda c: dot(recv_g[c], recv_r[c]), gl, gl_r, s_gl, r_gl)

    def copy_gc(t):
        at = pl.ds(pl.multiple_of(t * GROUP, GROUP), GROUP)
        return remote(gr_out.at[at], gr_in.at[at], s_gc.at[t], r_gc.at[t], other_core)

    def part_right(g, _):
        for q in range(GROUP):
            c = g * GROUP + q
            both = dot_tn(recv_g[c], recv_l[c])
            gr_own[c] = jnp.where(core == 0, both[:HALF], both[HALF:])
            gr_out[c] = jnp.where(core == 0, both[HALF:], both[:HALF]).astype(BF16)
        copy_gc(g).start()
        return 0

    lax.fori_loop(0, NG, part_right, 0)
    wait_recv(copy_gc, NG)
    copy_gr = exchange(lambda c: gr_own[c] + gr_in[c].astype(F32), gr, gr_r, s_gr, r_gr)

    def side_grad(b, ga, gb, out, src):
        widen(src)

        def project_grad(n, _):
            at = lanes(n, 2 * N)
            t = jnp.concatenate([half[pl.ds(2 * n + q, C, stride=ROWS), :] for q in range(2)], axis=1)
            gpt[2 * b * C : (2 * b + 1) * C, at] = (t * gb[:, at]).astype(BF16)
            gpt[(2 * b + 1) * C : (2 * b + 2) * C, at] = (t * ga[:, at]).astype(BF16)
            return 0

        lax.fori_loop(0, ROWS // 2, project_grad, 0)
        out[: 2 * C, :] = dot_nt(gpt[2 * b * C : (2 * b + 2) * C, :], xbf[...])

    def reduction(at, own, base, from_core, halves, from_xy, chunk, from_z):
        n = own.shape[0] // 2
        m = n // 16
        mine = pl.ds(pl.multiple_of(core * n, n), n)
        theirs = pl.ds(pl.multiple_of((1 - core) * n, n), n)
        final = sums.at[pl.ds(pl.multiple_of(base + core * n, n), n), :]

        def sem(k):
            return s_w.at[at, k], r_w.at[at, k]

        def scatter_core():
            return [remote(own.at[theirs, :], from_core, *sem(0), other_core)]

        def scatter_xy():
            copies = []
            for t in range(15):
                other, device = xy_peer(t)
                copies.append(remote(halves.at[pl.ds(pl.multiple_of(other * m, m), m), :], from_xy.at[my_xy], *sem(1 + t), device))
            return copies

        def exchange_z():
            return [remote(chunk.at[0], from_z.at[z], *sem(16 + t), z_peer(t)) for t in range(7)]

        def gather_xy():
            place_at = sums.at[pl.ds(pl.multiple_of(base + core * n + my_xy * m, m), m), :]
            return [remote(chunk.at[1], place_at, *sem(23 + t), xy_peer(t)[1]) for t in range(15)]

        def gather_core():
            return [remote(final, final, *sem(38), other_core)]

        steps = [scatter_core, scatter_xy, exchange_z, gather_xy, gather_core]

        def go(k):
            if k:
                for copy in steps[k - 1]():
                    copy.wait_recv()
            if k == 1:
                halves[...] = own[mine, :] + from_core[...]
                from_xy[my_xy] = halves[pl.ds(pl.multiple_of(my_xy * m, m), m), :]
            if k == 2:
                total = from_xy[0]
                for t in range(1, 16):
                    total = total + from_xy[t]
                chunk[0] = total
                from_z[z] = total
            if k == 3:
                total = from_z[0]
                for t in range(1, 8):
                    total = total + from_z[t]
                chunk[1] = total
                sums[pl.ds(pl.multiple_of(base + core * n + my_xy * m, m), m), :] = total
            if k < 5:
                for copy in steps[k]():
                    copy.start()

        def sent():
            for step in steps:
                for copy in step():
                    copy.wait_send()

        return go, sent

    def pair_part(n, _):
        at = lanes(n, 2 * N)
        dt[:, at] = dot(win[:, : 2 * C], gpt[: 2 * C, at]) + dot(win[:, 4 * C :], gpt[4 * C :, at])
        return 0

    def pair_grad(n, _):
        at = lanes(n, 2 * N)
        dx = dt[:, at] + dot(win[:, 2 * C : 4 * C], gpt[2 * C : 4 * C, at])
        xh = xhat[:, at]
        gx = scin[:, at] * (dx - mean0(dx) - xh * mean0(dx * xh))
        for q in range(2):
            gpair[2 * n + q] = gx[:, q * N : (q + 1) * N].T.astype(BF16)
        return 0

    go_early, sent_early = reduction(0, early, 0, e_core, e_half, e_xy, e_sum, e_z)
    go_late, sent_late = reduction(1, late, 4 * C, l_core, l_half, l_xy, l_sum, l_z)

    wait_recv(copy_gl, XP * NG)
    side_grad(0, al, bl, early, gl_r)
    go_early(0)
    lax.fori_loop(0, ROWS // 2, pair_part, 0)
    wait_recv(copy_gr, XP * NG)
    side_grad(1, ar, br, late, gr_r)
    go_late(0)
    go_early(1)
    go_late(1)
    lax.fori_loop(0, 2, pair_grad, 0)
    send_out(1)
    for n in range(1, 4):
        lax.fori_loop(2 * n, 2 * n + 2, pair_grad, 0)
        send_out(n + 1)
    go_early(2)
    go_late(2)
    go_early(3)
    go_late(3)
    go_early(4)
    go_late(4)
    go_early(5)
    go_late(5)

    for copy, count in (
        (copy_l, XP), (copy_r, XP), (copy_rc, NG), (copy_t, XP * NG), (copy_g, XP), (copy_gl, XP * NG), (copy_gc, NG), (copy_gr, XP * NG)
    ):
        wait_send(copy, count)
    sent_early()
    sent_late()

    @pl.when(swapped)
    def _():
        for n in range(6):
            swap_in(n).wait_send()
        for n in range(5):
            swap_out(n)[0].wait()

    @pl.when(jnp.logical_not(swapped))
    def _():
        for n in range(5):
            swap_out(n)[1].wait()


def finish(upd_in, gpair_in, sums, upd, gpair, gwin, gwout):
    upd[...] = upd_in[...]
    gpair[...] = gpair_in[...]
    whole = sums[...]
    squares = jnp.sum(jnp.sum(whole * whole, axis=0, keepdims=True), axis=1, keepdims=True)
    clip = jnp.minimum(1.0, lax.rsqrt(squares * (1.0 / (6 * C * C)) + 1e-06))
    for b, at in enumerate((0, 1, 4, 5, 2)):
        gwin[:, b * C : (b + 1) * C] = whole[at * C : (at + 1) * C].T * clip
    gwout[...] = whole[3 * C : 4 * C] * clip


def body(pair, pair_mask, cotangent, w_in, w_out):
    v = pltpu.VMEM
    dma = pltpu.SemaphoreType.DMA
    wide = v((C, WIDE), F32)
    wide_bf = v((C, WIDE), BF16)
    chan_half = v((CH, HALF, N), BF16)
    chan = v((CH, N, N), BF16)
    rows = v((C, ROWS, N), BF16)
    own = v((ROWS, N, C), BF16)
    blocks = v((4, CH, ROWS, N), BF16)

    def reduction(n):
        return [v((n // 2, C), F32), v((n // 2, C), F32), v((16, n // 32, C), F32), v((2, n // 32, C), F32), v((8, n // 32, C), F32)]

    scratch = [
        own, v((ROWS, N), jnp.int32), own, v((C, 5 * C), BF16), v((C, C), BF16), own, own,
        v((2, 4, 2 * CH, C), BF16), v((C, C), BF16), v((C, C), BF16),
        wide, wide_bf, v((1, WIDE), F32),
        v((2, 4, CH * ROWS, N), F32),
        blocks, blocks, chan_half, chan,
        wide, wide, wide, wide,
        wide, wide, wide_bf, wide, wide_bf, v((5 * C, WIDE), BF16),
        chan_half, rows, blocks, chan_half, v((C * ROWS, N), F32),
        chan_half, chan_half, v((CH, HALF, N), F32), chan_half, chan_half, rows, rows,
        v((4 * C, C), F32), v((2 * C, C), F32), v((C * ROWS, N), F32),
        *reduction(4 * C), *reduction(2 * C),
        dma((XP,)), dma((XP,)), dma((XP,)), dma((XP,)), dma((NG,)), dma((NG,)),
        dma((XP * NG,)), dma((XP * NG,)), dma((XP,)), dma((XP,)),
        dma((XP * NG,)), dma((XP * NG,)), dma((XP * NG,)), dma((XP * NG,)), dma((NG,)), dma((NG,)),
        dma((2, 39)), dma((2, 39)), dma((6,)), dma((6,)), dma((5,)), dma((5,)), dma((10,)),
    ]
    vm = pl.BlockSpec(memory_space=pltpu.VMEM)
    hbm = pl.BlockSpec(memory_space=pl.ANY)
    edges = jax.ShapeDtypeStruct((ROWS, N, C), BF16)
    update, grad_pair, sums = pl.pallas_call(
        kernel,
        name="triangle",
        out_shape=(edges, edges, jax.ShapeDtypeStruct((6 * C, C), F32)),
        in_specs=[hbm] * 5,
        out_specs=(hbm, hbm, vm),
        scratch_shapes=scratch,
        compiler_params=pltpu.CompilerParams(collective_id=0, has_side_effects=True, vmem_limit_bytes=56 * 2**20),
    )(pair[0], pair_mask[0], cotangent[0], w_in, w_out)
    update, grad_pair, grad_win, grad_wout = pl.pallas_call(
        finish,
        name="finish",
        out_shape=(edges, edges, jax.ShapeDtypeStruct((C, 5 * C), F32), jax.ShapeDtypeStruct((C, C), F32)),
        in_specs=[vm] * 3,
        out_specs=(vm,) * 4,
    )(update, grad_pair, sums)
    return update[None], grad_pair[None], grad_win, grad_wout


def solution(mesh):
    in_specs = (P("dp", "dap", None, None), P("dp", "dap", None), P("dp", "dap", None, None), P(), P())
    out_specs = (P("dp", "dap", None, None), P("dp", "dap", None, None), P(), P())
    return jax.shard_map(body, mesh=mesh, in_specs=in_specs, out_specs=out_specs, check_vma=False)
```

```python
import functools

import jax
import jax.numpy as jnp
from jax import lax
from jax.experimental import pallas as pl
from jax.experimental.pallas import tpu as pltpu
from jax.sharding import PartitionSpec as P

EPS = 1e-05
MESH = pl.DeviceIdType.MESH
F32 = jnp.float32
BF16 = jnp.bfloat16

C = 128
N = 128
ROWS = 16
CH = 32
HALF = N // 2
WIDE = ROWS * N
GROUP = 8
NG = CH // GROUP
XP = 3
XY = sorted(
    ((dx, dy) for dx in range(4) for dy in range(4) if dx or dy),
    key=lambda d: (-min(d[0], 4 - d[0]) - min(d[1], 4 - d[1]), d),
)
ZS = (4, 3, 5, 2, 6, 1, 7)


def dot(a, b):
    return lax.dot_general(a, b, (((1,), (0,)), ((), ())), preferred_element_type=F32)


def dot_nt(a, b):
    return lax.dot_general(a, b, (((1,), (1,)), ((), ())), preferred_element_type=F32)


def dot_tn(a, b):
    return lax.dot_general(a, b, (((0,), (0,)), ((), ())), preferred_element_type=F32)


def sigmoid(v):
    return 1.0 / (1.0 + jnp.exp(-v))


def mean0(v):
    return jnp.sum(v, axis=0, keepdims=True) * (1.0 / C)


def lanes(chunk, width):
    return pl.ds(pl.multiple_of(chunk * width, width), width)


def remote(src, dst, send_sem, recv_sem, device):
    return pltpu.make_async_remote_copy(
        src_ref=src, dst_ref=dst, send_sem=send_sem, recv_sem=recv_sem, device_id=device, device_id_type=MESH
    )


def kernel(
    pair_own, mask_own, cot_own, win_hbm, wout_hbm, upd_hbm, gpair_hbm, sums, pair, mask, cot, win, wout, upd, gpair,
    wt4, wog, woutt, xhat, xbf, scin, stage, send_l, send_r, recv_l, recv_r,
    al, bl, ar, br, ogs, a2, got, dt, tbt, gpt,
    tri, tri_r, send_g, recv_g, grad, gl, gr, gr_own, gr_out, gr_in, gl_r, gr_r, terms, half,
    from_core, halves, from_xy, chunk, from_z,
    s_l, r_l, s_r, r_r, s_rc, r_rc, s_t, r_t, s_g, r_g, s_gl, r_gl, s_gr, r_gr, s_gc, r_gc, s_w, r_w, s_in, r_in, s_out, r_out, io,
):
    dp, me = lax.axis_index("dp"), lax.axis_index("dap")
    zh, x = me // 4, me % 4
    y, zlo, core = dp // 8, (dp // 2) % 4, dp % 2

    z = zh * 4 + zlo

    swapped = core != zh

    def x_peer(t):
        return (x + 2 + t + t // 2) % 4

    def place(px, py, pz, pcore):
        return (py * 4 + pz % 4) * 2 + pcore, (pz // 4) * 4 + px

    def xy_peer(t):
        dx, dy = XY[t]
        px, py = (x + dx) % 4, (y + dy) % 4
        return py * 4 + px, place(px, py, z, core)

    def z_peer(t):
        return place(x, y, (z + ZS[t]) % 8, core)

    other_core = place(x, y, z, 1 - core)
    partner = place(x, y, (z + 4) % 8, 1 - core)

    def x_device(t):
        return place(x_peer(t), y, z, core)

    my_xy = y * 4 + x

    barrier = pltpu.get_barrier_semaphore()
    greet = [xy_peer(t)[1] for t in range(15)] + [z_peer(t) for t in range(7)] + [other_core]
    greet += [partner]
    for device in greet:
        pl.semaphore_signal(barrier, inc=1, device_id=device, device_id_type=MESH)

    def swap_in(n):
        if n < 4:
            src, dst = pair_own.at[pl.ds(4 * n, 4)], pair.at[pl.ds(4 * n, 4)]
        else:
            src, dst = ((mask_own, mask), (cot_own, cot))[n - 4]
        return remote(src, dst, s_in.at[n], r_in.at[n], partner)

    def keep_in(n):
        src, dst = ((pair_own, pair), (mask_own, mask), (cot_own, cot))[n]
        return pltpu.make_async_copy(src, dst, io.at[n])

    weights = [pltpu.make_async_copy(win_hbm, win, io.at[3]), pltpu.make_async_copy(wout_hbm, wout, io.at[4])]
    for copy in weights:
        copy.start()

    @pl.when(jnp.logical_not(swapped))
    def _():
        for n in range(3):
            keep_in(n).start()

    for copy in weights:
        copy.wait()
    for b in range(5):
        block = win[:, b * C : (b + 1) * C].astype(F32).T.astype(BF16)
        if b == 4:
            wog[...] = block
        else:
            for e in range(4):
                wt4[b // 2, e, (b % 2) * CH : (b % 2 + 1) * CH, :] = block[e * CH : (e + 1) * CH, :]
    woutt[...] = wout[...].astype(F32).T.astype(BF16)

    pl.semaphore_wait(barrier, 24)

    @pl.when(swapped)
    def _():
        for n in (4, 0, 1, 2, 3):
            swap_in(n).start()

    @pl.when(jnp.logical_not(swapped))
    def _():
        for n in range(3):
            keep_in(n).wait()


    def norm_pair(i, _):
        v = pair[i].astype(F32).T
        cen = v - mean0(v)
        sc = lax.rsqrt(mean0(cen * cen) + EPS)
        xh = cen * sc
        at = lanes(i, N)
        xhat[:, at] = xh
        xbf[:, at] = xh.astype(BF16)
        scin[:, at] = sc
        return 0

    def project(n):
        at = lanes(n, 4 * N)
        m = jnp.concatenate([mask[pl.ds(4 * n + q, 1), :] for q in range(4)], axis=1).astype(F32)
        for side, (ga, gb) in enumerate(((al, bl), (ar, br))):
            for e in range(4):
                rows = slice(e * CH, (e + 1) * CH)
                p = dot(wt4[side, e], xbf[:, at])
                s = sigmoid(p[:CH])
                sm = s * m
                v = sm * p[CH:]
                ga[rows, at] = sm
                gb[rows, at] = v * (1.0 - s)
                for q in range(4):
                    stage[side, e, pl.ds(4 * n + q, CH, stride=ROWS), :] = v[:, q * N : (q + 1) * N]

    for n in range(4):
        @pl.when(swapped)
        def _():
            if n == 0:
                swap_in(4).wait_recv()
            swap_in(n).wait_recv()
            if n == 3:
                swap_in(5).start()

        lax.fori_loop(4 * n, 4 * n + 4, norm_pair, 0, unroll=2)
        project(n)

    my_half = pl.ds(pl.multiple_of(core * HALF, HALF), HALF)
    my_rows = pl.ds(pl.multiple_of(core * HALF + x * ROWS, ROWS), ROWS)
    my_half_rows = pl.ds(pl.multiple_of(x * ROWS, ROWS), ROWS)
    my_ch = pl.multiple_of(x * CH, CH)

    def rounded(side, e):
        return stage[side, e].astype(BF16).reshape(CH, ROWS, N)

    def copy_r(t):
        return remote(send_r.at[x_peer(t)], recv_r.at[:, my_rows, :], s_r.at[t], r_r.at[t], x_device(t))

    def copy_l(t):
        return remote(send_l.at[x_peer(t)], recv_l.at[:, my_half_rows, :], s_l.at[t], r_l.at[t], x_device(t))

    def copy_rc(t):
        at = pl.ds(pl.multiple_of(t * GROUP, GROUP), GROUP)
        return remote(recv_r.at[at, my_half, :], recv_r.at[at, my_half, :], s_rc.at[t], r_rc.at[t], other_core)

    def send_right(t, _):
        e = x_peer(t)
        send_r[e] = rounded(1, e)
        copy_r(t).start()
        return 0

    def send_left(t, _):
        e = x_peer(t)
        send_l[e] = rounded(0, e)
        copy_l(t).start()
        return 0

    lax.fori_loop(0, XP, send_right, 0)
    lax.fori_loop(0, XP, send_left, 0)
    recv_r[:, my_rows, :] = rounded(1, x)
    recv_l[:, my_half_rows, :] = rounded(0, x)

    def gate(n, _):
        at = lanes(n, 2 * N)
        ogs[:, at] = sigmoid(dot(wog[...], xbf[:, at]))
        return 0

    lax.fori_loop(0, ROWS // 2, gate, 0)

    def gate_cot(n, _):
        at = lanes(n, 2 * N)
        og = ogs[:, at]
        g = jnp.concatenate([cot[2 * n].astype(F32).T, cot[2 * n + 1].astype(F32).T], axis=1)
        go = g * og
        gob = go.astype(BF16)
        a2[:, at] = go * (1.0 - og)
        got[:, at] = gob
        dt[:, at] = dot(wout[...], gob)
        return 0

    def wait_recv(copy, count):
        def one(t, _):
            copy(t).wait_recv()
            return 0

        lax.fori_loop(0, count, one, 0)

    def wait_send(copy, count):
        def one(t, _):
            copy(t).wait_send()
            return 0

        lax.fori_loop(0, count, one, 0)

    wait_recv(copy_r, XP)
    for t in range(NG):
        copy_rc(t).start()
    wait_recv(copy_l, XP)
    wait_recv(copy_rc, NG)

    def exchange(make, src, dst, ss, rs):
        def copy(t):
            g, k = t // XP, t % XP
            cs = pl.multiple_of(g * GROUP, GROUP)
            return remote(
                src.at[pl.ds(cs, GROUP), pl.ds(pl.multiple_of(x_peer(k) * ROWS, ROWS), ROWS), :],
                dst.at[pl.ds(my_ch + cs, GROUP), :, :],
                ss.at[t], rs.at[t], x_device(k),
            )

        def group(g, _):
            for q in range(GROUP):
                c = g * GROUP + q
                src[c] = make(c).astype(BF16)
            cs = pl.multiple_of(g * GROUP, GROUP)

            def start(t, _):
                copy(g * XP + t).start()
                return 0

            lax.fori_loop(0, XP, start, 0)
            dst[pl.ds(my_ch + cs, GROUP)] = src[pl.ds(cs, GROUP), my_half_rows, :]
            return 0

        lax.fori_loop(0, NG, group, 0)
        return copy

    def widen(src):
        def part(t, _):
            at = pl.ds(pl.multiple_of(t * 8, 8), 8)
            half[pl.ds(pl.multiple_of(t * N, N), N), :] = src[at].astype(F32).reshape(N, N)
            return 0

        lax.fori_loop(0, ROWS, part, 0, unroll=2)

    copy_t = exchange(lambda c: dot_nt(recv_l[c], recv_r[c]), tri, tri_r, s_t, r_t)

    @pl.when(swapped)
    def _():
        swap_in(5).wait_recv()

    lax.fori_loop(0, ROWS // 2, gate_cot, 0)
    wait_recv(copy_t, XP * NG)
    widen(tri_r)

    def rows_step(n, _):
        at = lanes(n, 2 * N)
        t = jnp.concatenate([half[pl.ds(2 * n + q, C, stride=ROWS), :] for q in range(2)], axis=1)
        cen = t - mean0(t)
        sc = lax.rsqrt(mean0(cen * cen) + EPS)
        tn = cen * sc
        tb = tn.astype(BF16)
        tbt[:, at] = tb
        out = dot(woutt[...], tb)
        u = ogs[:, at] * out
        gpt[4 * C :, at] = (a2[:, at] * out).astype(BF16)
        d = dt[:, at]
        gt = sc * (d - mean0(d) - tn * mean0(d * tn))
        for q in range(2):
            upd[2 * n + q] = u[:, q * N : (q + 1) * N].T.astype(BF16)
            grad[pl.ds(2 * n + q, C, stride=ROWS), :] = gt[:, q * N : (q + 1) * N]
        return 0

    lax.fori_loop(0, ROWS // 2, rows_step, 0)

    def swap_out(n):
        if n == 0:
            src, dst = upd, upd_hbm
        else:
            src, dst = gpair.at[pl.ds(4 * (n - 1), 4)], gpair_hbm.at[pl.ds(4 * (n - 1), 4)]
        return remote(src, dst, s_out.at[n], r_out.at[n], partner), pltpu.make_async_copy(src, dst, io.at[5 + n])

    def send_out(n):
        @pl.when(swapped)
        def _():
            swap_out(n)[0].start()

        @pl.when(jnp.logical_not(swapped))
        def _():
            swap_out(n)[1].start()

    send_out(0)

    def copy_g(t):
        return remote(send_g.at[x_peer(t)], recv_g.at[:, my_half_rows, :], s_g.at[t], r_g.at[t], x_device(t))

    def narrow(e):
        rows = pl.ds(pl.multiple_of(e * CH * ROWS, CH * ROWS), CH * ROWS)
        return grad[rows, :].astype(BF16).reshape(CH, ROWS, N)

    def start_g(t, _):
        e = x_peer(t)
        send_g[e] = narrow(e)
        copy_g(t).start()
        return 0

    lax.fori_loop(0, XP, start_g, 0)
    recv_g[:, my_half_rows, :] = narrow(x)

    terms[3 * C : 4 * C, :] = dot_nt(tbt[...], got[...])
    terms[2 * C : 3 * C, :] = dot_nt(gpt[4 * C :, :], xbf[...])

    wait_recv(copy_g, XP)
    copy_gl = exchange(lambda c: dot(recv_g[c], recv_r[c]), gl, gl_r, s_gl, r_gl)

    def copy_gc(t):
        at = pl.ds(pl.multiple_of(t * GROUP, GROUP), GROUP)
        return remote(gr_out.at[at], gr_in.at[at], s_gc.at[t], r_gc.at[t], other_core)

    def part_right(g, _):
        for q in range(GROUP):
            c = g * GROUP + q
            both = dot_tn(recv_g[c], recv_l[c])
            gr_own[c] = jnp.where(core == 0, both[:HALF], both[HALF:])
            gr_out[c] = jnp.where(core == 0, both[HALF:], both[:HALF]).astype(BF16)
        copy_gc(g).start()
        return 0

    lax.fori_loop(0, NG, part_right, 0)
    wait_recv(copy_gc, NG)
    copy_gr = exchange(lambda c: gr_own[c] + gr_in[c].astype(F32), gr, gr_r, s_gr, r_gr)

    def side_grad(b, ga, gb, src):
        widen(src)

        def project_grad(n, _):
            at = lanes(n, 2 * N)
            t = jnp.concatenate([half[pl.ds(2 * n + q, C, stride=ROWS), :] for q in range(2)], axis=1)
            gpt[2 * b * C : (2 * b + 1) * C, at] = (t * gb[:, at]).astype(BF16)
            gpt[(2 * b + 1) * C : (2 * b + 2) * C, at] = (t * ga[:, at]).astype(BF16)
            return 0

        lax.fori_loop(0, ROWS // 2, project_grad, 0)
        terms[4 * b * C : (4 * b + 2) * C, :] = dot_nt(gpt[2 * b * C : (2 * b + 2) * C, :], xbf[...])

    def reduction(own):
        n = own.shape[0] // 2
        m = n // 16
        mine = pl.ds(pl.multiple_of(core * n, n), n)
        theirs = pl.ds(pl.multiple_of((1 - core) * n, n), n)
        final = sums.at[pl.ds(pl.multiple_of(core * n, n), n), :]

        def sem(k):
            return s_w.at[k], r_w.at[k]

        def scatter_core():
            return [remote(own.at[theirs, :], from_core, *sem(0), other_core)]

        def scatter_xy():
            copies = []
            for t in range(15):
                other, device = xy_peer(t)
                copies.append(remote(halves.at[pl.ds(pl.multiple_of(other * m, m), m), :], from_xy.at[my_xy], *sem(1 + t), device))
            return copies

        def exchange_z():
            return [remote(chunk.at[0], from_z.at[z], *sem(16 + t), z_peer(t)) for t in range(7)]

        def gather_xy():
            place_at = sums.at[pl.ds(pl.multiple_of(core * n + my_xy * m, m), m), :]
            return [remote(chunk.at[1], place_at, *sem(23 + t), xy_peer(t)[1]) for t in range(15)]

        def gather_core():
            return [remote(final, final, *sem(38), other_core)]

        steps = [scatter_core, scatter_xy, exchange_z, gather_xy, gather_core]

        def go(k):
            if k:
                for copy in steps[k - 1]():
                    copy.wait_recv()
            if k == 1:
                halves[...] = own[mine, :] + from_core[...]
                from_xy[my_xy] = halves[pl.ds(pl.multiple_of(my_xy * m, m), m), :]
            if k == 2:
                total = from_xy[0]
                for t in range(1, 16):
                    total = total + from_xy[t]
                chunk[0] = total
                from_z[z] = total
            if k == 3:
                total = from_z[0]
                for t in range(1, 8):
                    total = total + from_z[t]
                chunk[1] = total
                sums[pl.ds(pl.multiple_of(core * n + my_xy * m, m), m), :] = total
            if k < 5:
                for copy in steps[k]():
                    copy.start()

        def sent():
            for step in steps:
                for copy in step():
                    copy.wait_send()

        return go, sent

    def pair_part(n, _):
        at = lanes(n, 2 * N)
        dt[:, at] = dot(win[:, : 2 * C], gpt[: 2 * C, at]) + dot(win[:, 4 * C :], gpt[4 * C :, at])
        return 0

    def pair_grad(n, _):
        at = lanes(n, 2 * N)
        dx = dt[:, at] + dot(win[:, 2 * C : 4 * C], gpt[2 * C : 4 * C, at])
        xh = xhat[:, at]
        gx = scin[:, at] * (dx - mean0(dx) - xh * mean0(dx * xh))
        for q in range(2):
            gpair[2 * n + q] = gx[:, q * N : (q + 1) * N].T.astype(BF16)
        return 0

    go, sent = reduction(terms)

    wait_recv(copy_gl, XP * NG)
    side_grad(0, al, bl, gl_r)
    lax.fori_loop(0, ROWS // 2, pair_part, 0)
    wait_recv(copy_gr, XP * NG)
    side_grad(1, ar, br, gr_r)
    go(0)
    for n in range(4):
        lax.fori_loop(2 * n, 2 * n + 2, pair_grad, 0)
        send_out(n + 1)
        if n == 0:
            go(1)
    for k in range(2, 6):
        go(k)

    for copy, count in (
        (copy_l, XP), (copy_r, XP), (copy_rc, NG), (copy_t, XP * NG), (copy_g, XP), (copy_gl, XP * NG), (copy_gc, NG), (copy_gr, XP * NG)
    ):
        wait_send(copy, count)
    sent()

    @pl.when(swapped)
    def _():
        for n in range(6):
            swap_in(n).wait_send()
        for n in range(5):
            swap_out(n)[0].wait()

    @pl.when(jnp.logical_not(swapped))
    def _():
        for n in range(5):
            swap_out(n)[1].wait()


def finish(upd_in, gpair_in, sums, upd, gpair, gwin, gwout):
    upd[...] = upd_in[...]
    gpair[...] = gpair_in[...]
    whole = sums[...]
    squares = jnp.sum(jnp.sum(whole * whole, axis=0, keepdims=True), axis=1, keepdims=True)
    clip = jnp.minimum(1.0, lax.rsqrt(squares * (1.0 / (6 * C * C)) + 1e-06))
    for b, at in enumerate((0, 1, 4, 5, 2)):
        gwin[:, b * C : (b + 1) * C] = whole[at * C : (at + 1) * C].T * clip
    gwout[...] = whole[3 * C : 4 * C] * clip


def body(pair, pair_mask, cotangent, w_in, w_out):
    v = pltpu.VMEM
    dma = pltpu.SemaphoreType.DMA
    wide = v((C, WIDE), F32)
    wide_bf = v((C, WIDE), BF16)
    chan_half = v((CH, HALF, N), BF16)
    chan = v((CH, N, N), BF16)
    rows = v((C, ROWS, N), BF16)
    own = v((ROWS, N, C), BF16)
    blocks = v((4, CH, ROWS, N), BF16)

    def reduction(n):
        return [v((n // 2, C), F32), v((n // 2, C), F32), v((16, n // 32, C), F32), v((2, n // 32, C), F32), v((8, n // 32, C), F32)]

    scratch = [
        own, v((ROWS, N), jnp.int32), own, v((C, 5 * C), BF16), v((C, C), BF16), own, own,
        v((2, 4, 2 * CH, C), BF16), v((C, C), BF16), v((C, C), BF16),
        wide, wide_bf, v((1, WIDE), F32),
        v((2, 4, CH * ROWS, N), F32),
        blocks, blocks, chan_half, chan,
        wide, wide, wide, wide,
        wide, wide, wide_bf, wide, wide_bf, v((5 * C, WIDE), BF16),
        chan_half, rows, blocks, chan_half, v((C * ROWS, N), F32),
        chan_half, chan_half, v((CH, HALF, N), F32), chan_half, chan_half, rows, rows,
        v((6 * C, C), F32), v((C * ROWS, N), F32),
        *reduction(6 * C),
        dma((XP,)), dma((XP,)), dma((XP,)), dma((XP,)), dma((NG,)), dma((NG,)),
        dma((XP * NG,)), dma((XP * NG,)), dma((XP,)), dma((XP,)),
        dma((XP * NG,)), dma((XP * NG,)), dma((XP * NG,)), dma((XP * NG,)), dma((NG,)), dma((NG,)),
        dma((39,)), dma((39,)), dma((6,)), dma((6,)), dma((5,)), dma((5,)), dma((10,)),
    ]
    vm = pl.BlockSpec(memory_space=pltpu.VMEM)
    hbm = pl.BlockSpec(memory_space=pl.ANY)
    edges = jax.ShapeDtypeStruct((ROWS, N, C), BF16)
    update, grad_pair, sums = pl.pallas_call(
        kernel,
        name="triangle",
        out_shape=(edges, edges, jax.ShapeDtypeStruct((6 * C, C), F32)),
        in_specs=[hbm] * 5,
        out_specs=(hbm, hbm, vm),
        scratch_shapes=scratch,
        compiler_params=pltpu.CompilerParams(collective_id=0, has_side_effects=True, vmem_limit_bytes=56 * 2**20),
    )(pair[0], pair_mask[0], cotangent[0], w_in, w_out)
    update, grad_pair, grad_win, grad_wout = pl.pallas_call(
        finish,
        name="finish",
        out_shape=(edges, edges, jax.ShapeDtypeStruct((C, 5 * C), F32), jax.ShapeDtypeStruct((C, C), F32)),
        in_specs=[vm] * 3,
        out_specs=(vm,) * 4,
    )(update, grad_pair, sums)
    return update[None], grad_pair[None], grad_win, grad_wout


def solution(mesh):
    in_specs = (P("dp", "dap", None, None), P("dp", "dap", None), P("dp", "dap", None, None), P(), P())
    out_specs = (P("dp", "dap", None, None), P("dp", "dap", None, None), P(), P())
    return jax.shard_map(body, mesh=mesh, in_specs=in_specs, out_specs=out_specs, check_vma=False)
```

```python
import functools

import jax
import jax.numpy as jnp
from jax import lax
from jax.experimental import pallas as pl
from jax.experimental.pallas import tpu as pltpu
from jax.sharding import PartitionSpec as P

EPS = 1e-05
MESH = pl.DeviceIdType.MESH
F32 = jnp.float32
BF16 = jnp.bfloat16

C = 128
N = 128
ROWS = 16
CH = 32
HALF = N // 2
WIDE = ROWS * N
GROUP = 8
NG = CH // GROUP
XP = 3
XY = sorted(
    ((dx, dy) for dx in range(4) for dy in range(4) if dx or dy),
    key=lambda d: (-min(d[0], 4 - d[0]) - min(d[1], 4 - d[1]), d),
)
ZS = (4, 3, 5, 2, 6, 1, 7)


def dot(a, b):
    return lax.dot_general(a, b, (((1,), (0,)), ((), ())), preferred_element_type=F32)


def dot_nt(a, b):
    return lax.dot_general(a, b, (((1,), (1,)), ((), ())), preferred_element_type=F32)


def dot_tn(a, b):
    return lax.dot_general(a, b, (((0,), (0,)), ((), ())), preferred_element_type=F32)


def sigmoid(v):
    return 1.0 / (1.0 + jnp.exp(-v))


def mean0(v):
    return jnp.sum(v, axis=0, keepdims=True) * (1.0 / C)


def lanes(chunk, width):
    return pl.ds(pl.multiple_of(chunk * width, width), width)


def remote(src, dst, send_sem, recv_sem, device):
    return pltpu.make_async_remote_copy(
        src_ref=src, dst_ref=dst, send_sem=send_sem, recv_sem=recv_sem, device_id=device, device_id_type=MESH
    )


def kernel(
    pair_own, mask_own, cot_own, win_hbm, wout_hbm, upd_hbm, gpair_hbm, sums, pair, mask, cot, win, wout, upd, gpair,
    wt4, wog, woutt, xhat, xbf, scin, stage, send_l, send_r, recv_l, recv_r,
    al, bl, ar, br, ogs, a2, got, dt, tbt, gpt,
    tri, tri_r, send_g, recv_g, grad, gl, gr, gr_own, gr_out, gr_in, gl_r, gr_r, terms, half,
    from_core, halves, from_xy, chunk, from_z,
    s_l, r_l, s_r, r_r, s_rc, r_rc, s_t, r_t, s_g, r_g, s_gl, r_gl, s_gr, r_gr, s_gc, r_gc, s_w, r_w, s_in, r_in, s_out, r_out, io,
):
    dp, me = lax.axis_index("dp"), lax.axis_index("dap")
    zh, x = me // 4, me % 4
    y, zlo, core = dp // 8, (dp // 2) % 4, dp % 2

    z = zh * 4 + zlo

    swapped = core != zh

    def x_peer(t):
        return (x + 2 + t + t // 2) % 4

    def place(px, py, pz, pcore):
        return (py * 4 + pz % 4) * 2 + pcore, (pz // 4) * 4 + px

    def xy_peer(t):
        dx, dy = XY[t]
        px, py = (x + dx) % 4, (y + dy) % 4
        return py * 4 + px, place(px, py, z, core)

    def z_peer(t):
        return place(x, y, (z + ZS[t]) % 8, core)

    other_core = place(x, y, z, 1 - core)
    partner = place(x, y, (z + 4) % 8, 1 - core)

    def x_device(t):
        return place(x_peer(t), y, z, core)

    my_xy = y * 4 + x

    barrier = pltpu.get_barrier_semaphore()
    greet = [xy_peer(t)[1] for t in range(15)] + [z_peer(t) for t in range(7)] + [other_core]
    greet += [partner]
    for device in greet:
        pl.semaphore_signal(barrier, inc=1, device_id=device, device_id_type=MESH)

    def swap_in(n):
        if n < 4:
            src, dst = pair_own.at[pl.ds(4 * n, 4)], pair.at[pl.ds(4 * n, 4)]
        else:
            src, dst = ((mask_own, mask), (cot_own, cot))[n - 4]
        return remote(src, dst, s_in.at[n], r_in.at[n], partner)

    def keep_in(n):
        src, dst = ((pair_own, pair), (mask_own, mask), (cot_own, cot))[n]
        return pltpu.make_async_copy(src, dst, io.at[n])

    weights = [pltpu.make_async_copy(win_hbm, win, io.at[3]), pltpu.make_async_copy(wout_hbm, wout, io.at[4])]
    for copy in weights:
        copy.start()

    @pl.when(jnp.logical_not(swapped))
    def _():
        for n in range(3):
            keep_in(n).start()

    for copy in weights:
        copy.wait()
    for b in range(5):
        block = win[:, b * C : (b + 1) * C].astype(F32).T.astype(BF16)
        if b == 4:
            wog[...] = block
        else:
            for e in range(4):
                wt4[b // 2, e, (b % 2) * CH : (b % 2 + 1) * CH, :] = block[e * CH : (e + 1) * CH, :]
    woutt[...] = wout[...].astype(F32).T.astype(BF16)

    pl.semaphore_wait(barrier, 24)

    @pl.when(swapped)
    def _():
        for n in (4, 0, 1, 2, 3):
            swap_in(n).start()

    @pl.when(jnp.logical_not(swapped))
    def _():
        for n in range(3):
            keep_in(n).wait()


    def norm_pair(i, _):
        v = pair[i].astype(F32).T
        cen = v - mean0(v)
        sc = lax.rsqrt(mean0(cen * cen) + EPS)
        xh = cen * sc
        at = lanes(i, N)
        xhat[:, at] = xh
        xbf[:, at] = xh.astype(BF16)
        scin[:, at] = sc
        return 0

    def project(n):
        at = lanes(n, 4 * N)
        m = jnp.concatenate([mask[pl.ds(4 * n + q, 1), :] for q in range(4)], axis=1).astype(F32)
        for side, (ga, gb) in enumerate(((al, bl), (ar, br))):
            for e in range(4):
                rows = slice(e * CH, (e + 1) * CH)
                p = dot(wt4[side, e], xbf[:, at])
                s = sigmoid(p[:CH])
                sm = s * m
                v = sm * p[CH:]
                ga[rows, at] = sm
                gb[rows, at] = v * (1.0 - s)
                for q in range(4):
                    stage[side, e, pl.ds(4 * n + q, CH, stride=ROWS), :] = v[:, q * N : (q + 1) * N]

    for n in range(4):
        @pl.when(swapped)
        def _():
            if n == 0:
                swap_in(4).wait_recv()
            swap_in(n).wait_recv()
            if n == 3:
                swap_in(5).start()

        lax.fori_loop(4 * n, 4 * n + 4, norm_pair, 0, unroll=2)
        project(n)

    my_half = pl.ds(pl.multiple_of(core * HALF, HALF), HALF)
    my_rows = pl.ds(pl.multiple_of(core * HALF + x * ROWS, ROWS), ROWS)
    my_half_rows = pl.ds(pl.multiple_of(x * ROWS, ROWS), ROWS)
    my_ch = pl.multiple_of(x * CH, CH)

    def rounded(side, e):
        return stage[side, e].astype(BF16).reshape(CH, ROWS, N)

    def copy_r(t):
        return remote(send_r.at[x_peer(t)], recv_r.at[:, my_rows, :], s_r.at[t], r_r.at[t], x_device(t))

    def copy_l(t):
        return remote(send_l.at[x_peer(t)], recv_l.at[:, my_half_rows, :], s_l.at[t], r_l.at[t], x_device(t))

    def copy_rc(t):
        at = pl.ds(pl.multiple_of(t * GROUP, GROUP), GROUP)
        return remote(recv_r.at[at, my_half, :], recv_r.at[at, my_half, :], s_rc.at[t], r_rc.at[t], other_core)

    def send_right(t, _):
        e = x_peer(t)
        send_r[e] = rounded(1, e)
        copy_r(t).start()
        return 0

    def send_left(t, _):
        e = x_peer(t)
        send_l[e] = rounded(0, e)
        copy_l(t).start()
        return 0

    lax.fori_loop(0, XP, send_right, 0)
    lax.fori_loop(0, XP, send_left, 0)
    recv_r[:, my_rows, :] = rounded(1, x)
    recv_l[:, my_half_rows, :] = rounded(0, x)

    def gate(n, _):
        at = lanes(n, 2 * N)
        ogs[:, at] = sigmoid(dot(wog[...], xbf[:, at]))
        return 0

    lax.fori_loop(0, ROWS // 2, gate, 0)

    def gate_cot(n, _):
        at = lanes(n, 2 * N)
        og = ogs[:, at]
        g = jnp.concatenate([cot[2 * n].astype(F32).T, cot[2 * n + 1].astype(F32).T], axis=1)
        go = g * og
        gob = go.astype(BF16)
        a2[:, at] = go * (1.0 - og)
        got[:, at] = gob
        dt[:, at] = dot(wout[...], gob)
        return 0

    def wait_recv(copy, count):
        def one(t, _):
            copy(t).wait_recv()
            return 0

        lax.fori_loop(0, count, one, 0)

    def wait_send(copy, count):
        def one(t, _):
            copy(t).wait_send()
            return 0

        lax.fori_loop(0, count, one, 0)

    wait_recv(copy_r, XP)
    for t in range(NG):
        copy_rc(t).start()
    wait_recv(copy_l, XP)
    wait_recv(copy_rc, NG)

    def exchange(make, src, dst, ss, rs):
        def copy(t):
            g, k = t // XP, t % XP
            cs = pl.multiple_of(g * GROUP, GROUP)
            return remote(
                src.at[pl.ds(cs, GROUP), pl.ds(pl.multiple_of(x_peer(k) * ROWS, ROWS), ROWS), :],
                dst.at[pl.ds(my_ch + cs, GROUP), :, :],
                ss.at[t], rs.at[t], x_device(k),
            )

        def group(g, _):
            for q in range(GROUP):
                c = g * GROUP + q
                src[c] = make(c).astype(BF16)
            cs = pl.multiple_of(g * GROUP, GROUP)

            def start(t, _):
                copy(g * XP + t).start()
                return 0

            lax.fori_loop(0, XP, start, 0)
            dst[pl.ds(my_ch + cs, GROUP)] = src[pl.ds(cs, GROUP), my_half_rows, :]
            return 0

        lax.fori_loop(0, NG, group, 0)
        return copy

    def widen(src):
        def part(t, _):
            at = pl.ds(pl.multiple_of(t * 8, 8), 8)
            half[pl.ds(pl.multiple_of(t * N, N), N), :] = src[at].astype(F32).reshape(N, N)
            return 0

        lax.fori_loop(0, ROWS, part, 0, unroll=2)

    copy_t = exchange(lambda c: dot_nt(recv_l[c], recv_r[c]), tri, tri_r, s_t, r_t)

    @pl.when(swapped)
    def _():
        swap_in(5).wait_recv()

    lax.fori_loop(0, ROWS // 2, gate_cot, 0)
    wait_recv(copy_t, XP * NG)
    widen(tri_r)

    def rows_step(n, _):
        at = lanes(n, 2 * N)
        t = jnp.concatenate([half[pl.ds(2 * n + q, C, stride=ROWS), :] for q in range(2)], axis=1)
        cen = t - mean0(t)
        sc = lax.rsqrt(mean0(cen * cen) + EPS)
        tn = cen * sc
        tb = tn.astype(BF16)
        tbt[:, at] = tb
        out = dot(woutt[...], tb)
        u = ogs[:, at] * out
        gpt[4 * C :, at] = (a2[:, at] * out).astype(BF16)
        d = dt[:, at]
        gt = sc * (d - mean0(d) - tn * mean0(d * tn))
        for q in range(2):
            upd[2 * n + q] = u[:, q * N : (q + 1) * N].T.astype(BF16)
            grad[pl.ds(2 * n + q, C, stride=ROWS), :] = gt[:, q * N : (q + 1) * N]
        return 0

    lax.fori_loop(0, ROWS // 2, rows_step, 0)

    def swap_out(n):
        if n == 0:
            src, dst = upd, upd_hbm
        else:
            src, dst = gpair.at[pl.ds(4 * (n - 1), 4)], gpair_hbm.at[pl.ds(4 * (n - 1), 4)]
        return remote(src, dst, s_out.at[n], r_out.at[n], partner), pltpu.make_async_copy(src, dst, io.at[5 + n])

    def send_out(n):
        @pl.when(swapped)
        def _():
            swap_out(n)[0].start()

        @pl.when(jnp.logical_not(swapped))
        def _():
            swap_out(n)[1].start()

    send_out(0)

    def copy_g(t):
        return remote(send_g.at[x_peer(t)], recv_g.at[:, my_half_rows, :], s_g.at[t], r_g.at[t], x_device(t))

    def narrow(e):
        rows = pl.ds(pl.multiple_of(e * CH * ROWS, CH * ROWS), CH * ROWS)
        return grad[rows, :].astype(BF16).reshape(CH, ROWS, N)

    def start_g(t, _):
        e = x_peer(t)
        send_g[e] = narrow(e)
        copy_g(t).start()
        return 0

    lax.fori_loop(0, XP, start_g, 0)
    recv_g[:, my_half_rows, :] = narrow(x)

    terms[3 * C : 4 * C, :] = dot_nt(tbt[...], got[...])
    terms[2 * C : 3 * C, :] = dot_nt(gpt[4 * C :, :], xbf[...])

    wait_recv(copy_g, XP)

    def copy_gc(t):
        at = pl.ds(pl.multiple_of(t * GROUP, GROUP), GROUP)
        return remote(gr_out.at[at], gr_in.at[at], s_gc.at[t], r_gc.at[t], other_core)

    def part_right(g, _):
        for q in range(GROUP):
            c = g * GROUP + q
            both = dot_tn(recv_g[c], recv_l[c])
            gr_own[c] = jnp.where(core == 0, both[:HALF], both[HALF:])
            gr_out[c] = jnp.where(core == 0, both[HALF:], both[:HALF]).astype(BF16)
        copy_gc(g).start()
        return 0

    lax.fori_loop(0, NG, part_right, 0)
    copy_gl = exchange(lambda c: dot(recv_g[c], recv_r[c]), gl, gl_r, s_gl, r_gl)
    wait_recv(copy_gc, NG)
    copy_gr = exchange(lambda c: gr_own[c] + gr_in[c].astype(F32), gr, gr_r, s_gr, r_gr)

    def side_grad(b, ga, gb, src):
        widen(src)

        def project_grad(n, _):
            at = lanes(n, 2 * N)
            t = jnp.concatenate([half[pl.ds(2 * n + q, C, stride=ROWS), :] for q in range(2)], axis=1)
            gpt[2 * b * C : (2 * b + 1) * C, at] = (t * gb[:, at]).astype(BF16)
            gpt[(2 * b + 1) * C : (2 * b + 2) * C, at] = (t * ga[:, at]).astype(BF16)
            return 0

        lax.fori_loop(0, ROWS // 2, project_grad, 0)
        terms[4 * b * C : (4 * b + 2) * C, :] = dot_nt(gpt[2 * b * C : (2 * b + 2) * C, :], xbf[...])

    def reduction(own):
        n = own.shape[0] // 2
        m = n // 16
        mine = pl.ds(pl.multiple_of(core * n, n), n)
        theirs = pl.ds(pl.multiple_of((1 - core) * n, n), n)
        final = sums.at[pl.ds(pl.multiple_of(core * n, n), n), :]

        def sem(k):
            return s_w.at[k], r_w.at[k]

        def scatter_core():
            return [remote(own.at[theirs, :], from_core, *sem(0), other_core)]

        def scatter_xy():
            copies = []
            for t in range(15):
                other, device = xy_peer(t)
                copies.append(remote(halves.at[pl.ds(pl.multiple_of(other * m, m), m), :], from_xy.at[my_xy], *sem(1 + t), device))
            return copies

        def exchange_z():
            return [remote(chunk.at[0], from_z.at[z], *sem(16 + t), z_peer(t)) for t in range(7)]

        def gather_xy():
            place_at = sums.at[pl.ds(pl.multiple_of(core * n + my_xy * m, m), m), :]
            return [remote(chunk.at[1], place_at, *sem(23 + t), xy_peer(t)[1]) for t in range(15)]

        def gather_core():
            return [remote(final, final, *sem(38), other_core)]

        steps = [scatter_core, scatter_xy, exchange_z, gather_xy, gather_core]

        def go(k):
            if k:
                for copy in steps[k - 1]():
                    copy.wait_recv()
            if k == 1:
                halves[...] = own[mine, :] + from_core[...]
                from_xy[my_xy] = halves[pl.ds(pl.multiple_of(my_xy * m, m), m), :]
            if k == 2:
                total = from_xy[0]
                for t in range(1, 16):
                    total = total + from_xy[t]
                chunk[0] = total
                from_z[z] = total
            if k == 3:
                total = from_z[0]
                for t in range(1, 8):
                    total = total + from_z[t]
                chunk[1] = total
                sums[pl.ds(pl.multiple_of(core * n + my_xy * m, m), m), :] = total
            if k < 5:
                for copy in steps[k]():
                    copy.start()

        def sent():
            for step in steps:
                for copy in step():
                    copy.wait_send()

        return go, sent

    def pair_part(n, _):
        at = lanes(n, 2 * N)
        dt[:, at] = dot(win[:, : 2 * C], gpt[: 2 * C, at]) + dot(win[:, 4 * C :], gpt[4 * C :, at])
        return 0

    def pair_grad(n, _):
        at = lanes(n, 2 * N)
        dx = dt[:, at] + dot(win[:, 2 * C : 4 * C], gpt[2 * C : 4 * C, at])
        xh = xhat[:, at]
        gx = scin[:, at] * (dx - mean0(dx) - xh * mean0(dx * xh))
        for q in range(2):
            gpair[2 * n + q] = gx[:, q * N : (q + 1) * N].T.astype(BF16)
        return 0

    go, sent = reduction(terms)

    wait_recv(copy_gl, XP * NG)
    side_grad(0, al, bl, gl_r)
    lax.fori_loop(0, ROWS // 2, pair_part, 0)
    wait_recv(copy_gr, XP * NG)
    side_grad(1, ar, br, gr_r)
    go(0)
    for n in range(4):
        lax.fori_loop(2 * n, 2 * n + 2, pair_grad, 0)
        send_out(n + 1)
        if n == 0:
            go(1)
    for k in range(2, 6):
        go(k)

    for copy, count in (
        (copy_l, XP), (copy_r, XP), (copy_rc, NG), (copy_t, XP * NG), (copy_g, XP), (copy_gl, XP * NG), (copy_gc, NG), (copy_gr, XP * NG)
    ):
        wait_send(copy, count)
    sent()

    @pl.when(swapped)
    def _():
        for n in range(6):
            swap_in(n).wait_send()
        for n in range(5):
            swap_out(n)[0].wait()

    @pl.when(jnp.logical_not(swapped))
    def _():
        for n in range(5):
            swap_out(n)[1].wait()


def finish(upd_in, gpair_in, sums, upd, gpair, gwin, gwout):
    upd[...] = upd_in[...]
    gpair[...] = gpair_in[...]
    whole = sums[...]
    squares = jnp.sum(jnp.sum(whole * whole, axis=0, keepdims=True), axis=1, keepdims=True)
    clip = jnp.minimum(1.0, lax.rsqrt(squares * (1.0 / (6 * C * C)) + 1e-06))
    for b, at in enumerate((0, 1, 4, 5, 2)):
        gwin[:, b * C : (b + 1) * C] = whole[at * C : (at + 1) * C].T * clip
    gwout[...] = whole[3 * C : 4 * C] * clip


def body(pair, pair_mask, cotangent, w_in, w_out):
    v = pltpu.VMEM
    dma = pltpu.SemaphoreType.DMA
    wide = v((C, WIDE), F32)
    wide_bf = v((C, WIDE), BF16)
    chan_half = v((CH, HALF, N), BF16)
    chan = v((CH, N, N), BF16)
    rows = v((C, ROWS, N), BF16)
    own = v((ROWS, N, C), BF16)
    blocks = v((4, CH, ROWS, N), BF16)

    def reduction(n):
        return [v((n // 2, C), F32), v((n // 2, C), F32), v((16, n // 32, C), F32), v((2, n // 32, C), F32), v((8, n // 32, C), F32)]

    scratch = [
        own, v((ROWS, N), jnp.int32), own, v((C, 5 * C), BF16), v((C, C), BF16), own, own,
        v((2, 4, 2 * CH, C), BF16), v((C, C), BF16), v((C, C), BF16),
        wide, wide_bf, v((1, WIDE), F32),
        v((2, 4, CH * ROWS, N), F32),
        blocks, blocks, chan_half, chan,
        wide, wide, wide, wide,
        wide, wide, wide_bf, wide, wide_bf, v((5 * C, WIDE), BF16),
        chan_half, rows, blocks, chan_half, v((C * ROWS, N), F32),
        chan_half, chan_half, v((CH, HALF, N), F32), chan_half, chan_half, rows, rows,
        v((6 * C, C), F32), v((C * ROWS, N), F32),
        *reduction(6 * C),
        dma((XP,)), dma((XP,)), dma((XP,)), dma((XP,)), dma((NG,)), dma((NG,)),
        dma((XP * NG,)), dma((XP * NG,)), dma((XP,)), dma((XP,)),
        dma((XP * NG,)), dma((XP * NG,)), dma((XP * NG,)), dma((XP * NG,)), dma((NG,)), dma((NG,)),
        dma((39,)), dma((39,)), dma((6,)), dma((6,)), dma((5,)), dma((5,)), dma((10,)),
    ]
    vm = pl.BlockSpec(memory_space=pltpu.VMEM)
    hbm = pl.BlockSpec(memory_space=pl.ANY)
    edges = jax.ShapeDtypeStruct((ROWS, N, C), BF16)
    update, grad_pair, sums = pl.pallas_call(
        kernel,
        name="triangle",
        out_shape=(edges, edges, jax.ShapeDtypeStruct((6 * C, C), F32)),
        in_specs=[hbm] * 5,
        out_specs=(hbm, hbm, vm),
        scratch_shapes=scratch,
        compiler_params=pltpu.CompilerParams(collective_id=0, has_side_effects=True, vmem_limit_bytes=56 * 2**20),
    )(pair[0], pair_mask[0], cotangent[0], w_in, w_out)
    update, grad_pair, grad_win, grad_wout = pl.pallas_call(
        finish,
        name="finish",
        out_shape=(edges, edges, jax.ShapeDtypeStruct((C, 5 * C), F32), jax.ShapeDtypeStruct((C, C), F32)),
        in_specs=[vm] * 3,
        out_specs=(vm,) * 4,
    )(update, grad_pair, sums)
    return update[None], grad_pair[None], grad_win, grad_wout


def solution(mesh):
    in_specs = (P("dp", "dap", None, None), P("dp", "dap", None), P("dp", "dap", None, None), P(), P())
    out_specs = (P("dp", "dap", None, None), P("dp", "dap", None, None), P(), P())
    return jax.shard_map(body, mesh=mesh, in_specs=in_specs, out_specs=out_specs, check_vma=False)
```
